128 devices in a mesh: ctx: 32 (over x_lo, y, z), tp: 4 (over x_hi, core).
Axes of the slice: x: 4 (x_hi: 2, x_lo: 2; x = x_hi * 2 + x_lo), y: 4, z: 4, core: 2. Of those that a mesh axis runs over, the one named last changes fastest.
Arguments:
- q_pre: bfloat16 [8192, 4096], P('ctx', 'tp'), may hold values from -20 to 20
- prefill_key_value: bfloat16 [2, 8192, 512], P(None, 'ctx', 'tp'), may hold values from -20 to 20
- kv_past: bfloat16 [2, 8192, 512], P(None, 'ctx', 'tp'), may hold values from -20 to 20
- offset: int32 [1], replicated, may hold values from 4096 to 8192
- page_dest: int32 [512, 1], P('ctx'), may hold values from 0 to 31; in each aligned block of 16 rows (0 to 15, 16 to 31, ...) at most 2 rows name the same one
- slot_perm: int32 [32, 64], P('ctx'), may hold values from 0 to 63, each once within a row
- pool: bfloat16 [2, 32768, 512], P(None, 'ctx', 'tp'), may hold values from -20 to 20
- tables: int32 [2048, 32], P('ctx'), may hold values from 0 to 63
- lengths: int32 [32, 64], P('ctx'), may hold values from 1 to 512, 16384 in all within a row
- decode_query: bfloat16 [2048, 4, 4096], P('ctx', None, 'tp'), may hold values from -20 to 20
- decode_key_value: bfloat16 [2, 2048, 4, 512], P(None, 'ctx', None, 'tp'), may hold values from -4 to 4
- out_weight: bfloat16 [4096, 8192], P('tp'), may hold values from -0.375 to 0.375
Outputs:
- pre_out: bfloat16 [8192, 4096], P('ctx', 'tp')
- handed_pools: bfloat16 [2, 32768, 512], P(None, 'ctx', 'tp')
- dec_out: bfloat16 [2048, 4, 8192], P(('ctx', 'tp'))
The draws below stay inside these ranges and needn't reach their ends.
Inputs may be any that keep to these rules, and one draw needn't show every extreme that they name: `page_dest`: among the 16 pages of one index of ctx at most 2 name the same decode instance, and in every draw some index sends exactly 2 pages to one instance. `slot_perm`: each row is a permutation of the 64 slots. Each instance's lengths sum to 16384 and the longest is exactly 512.
All inputs are finite; a program needn't handle non-finite values.
Results may differ from the reference program's by a relative error of at most 0.015.
Values may be sent and summed in bfloat16 or wider, within the bound.
No kernel may reach another device: no remote copies, remote signals or barrier semaphores. Data moves between devices by JAX's collectives and lax.ppermute only.
A program may use at most 128 MiB of HBM per device.

```python
import math
import jax
import jax.numpy as jnp
import numpy as np
from jax import lax

D = 8192
QUERY_HEADS = 32
KEY_VALUE_HEADS = 4
HEAD_SIZE = 128
PAGE_TOKENS = 16
CAP = 2
INSTANCE_ROWS = 64
ROW_PAGES = 32
DECODE_STEPS = 4
STRETCH_TOKENS = 8192
PREFIX_TOKENS = 8192
PAGES_DEV = 16
STRETCH_PAGES = 512
POOL_SLOTS = 64
POOL_TOKEN_ROWS = 32768
DECODE_ROWS = 2048
N_CTX = 32


def draw_q_pre(key, part):
    key = jax.random.fold_in(key, 11)
    value_rows = jnp.clip(jax.random.normal(key, (STRETCH_TOKENS, QUERY_HEADS * HEAD_SIZE), jnp.float32), -4.0, 4.0)
    return value_rows.astype(jnp.bfloat16)


def draw_prefill_key_value(key, part):
    key = jax.random.fold_in(key, 12)
    value_rows = jnp.clip(jax.random.normal(key, (2, STRETCH_TOKENS, KEY_VALUE_HEADS * HEAD_SIZE), jnp.float32), -4.0, 4.0)
    return value_rows.astype(jnp.bfloat16)


def draw_kv_past(key, part):
    key = jax.random.fold_in(key, 13)
    value_rows = jnp.clip(jax.random.normal(key, (2, PREFIX_TOKENS, KEY_VALUE_HEADS * HEAD_SIZE), jnp.float32), -4.0, 4.0)
    return value_rows.astype(jnp.bfloat16)


def draw_pool(key, part):
    key = jax.random.fold_in(key, 14)
    value_rows = jnp.clip(jax.random.normal(key, (2, POOL_TOKEN_ROWS, KEY_VALUE_HEADS * HEAD_SIZE), jnp.float32), -4.0, 4.0)
    return value_rows.astype(jnp.bfloat16)


def draw_decode_query(key, part):
    key = jax.random.fold_in(key, 15)
    value_rows = jnp.clip(jax.random.normal(key, (DECODE_ROWS, DECODE_STEPS, QUERY_HEADS * HEAD_SIZE), jnp.float32), -4.0, 4.0)
    return value_rows.astype(jnp.bfloat16)


def touch_ends(array, stream_key, low, high):
    index_at = [jax.random.randint(jax.random.fold_in(stream_key, axis), (), 0, length) for axis, length in enumerate(array.shape)]
    main_axis = array.shape.index(max(array.shape))
    neighbour = index_at[:main_axis] + [(index_at[main_axis] + 1) % array.shape[main_axis]] + index_at[main_axis + 1:]
    return array.at[tuple(index_at)].set(low).at[tuple(neighbour)].set(high)


def block_levels(stream_key, dims, cuts, smallest, largest):
    def one(dim, shards_of):
        heights = jax.random.uniform(jax.random.fold_in(jax.random.fold_in(stream_key, 6), dim), (shards_of,), jnp.float32, smallest / len(cuts), largest / len(cuts))
        return jnp.repeat(jnp.exp(heights), dims[dim] // shards_of).reshape((-1,) + (1,) * (len(dims) - dim - 1))

    loudness = one(*cuts[0])
    for cut in cuts[1:]:
        loudness = loudness * one(*cut)
    return loudness


def split_up(number_of, total, bound, skew):
    loads = [(1 << 20) // math.isqrt(grade ** skew) + 1 for grade in range(2, number_of + 1)]
    surplus, holding = total - bound - (number_of - 1), [1] * (number_of - 1)
    while surplus > 0:
        movable = [i for i in range(number_of - 1) if holding[i] < bound]
        mass, remaining = sum([loads[i] for i in movable]), surplus
        for i in movable:
            more = min(bound - holding[i], max(1, remaining * loads[i] // mass), surplus)
            holding[i] = holding[i] + more
            surplus = surplus - more
    return np.array([bound] + holding)


def ragged_sizes(rng, count, total, most, skew):
    if count == 2:
        one = jax.random.randint(rng, (), max(1, total - most), min(most, total - 1) + 1)
        return jnp.stack([one, total - one])
    sizes = jnp.asarray(split_up(count, total, most, skew), jnp.int32)
    twos = (count - 1) // 2
    giver, receiver = sizes[1:1 + 2 * twos:2], sizes[2:2 + 2 * twos:2]
    room = jnp.minimum(giver - 1, most - receiver)
    shifted = jax.random.randint(jax.random.fold_in(rng, 1), (twos,), 0, 1 << 20) % (room + 1)
    sizes = sizes.at[1:1 + 2 * twos:2].set(giver - shifted).at[2:2 + 2 * twos:2].set(receiver + shifted)
    return sizes[jax.random.permutation(jax.random.fold_in(rng, 2), count)]


def deal_out(key, own, number, rows, number_of, top, most, skew):
    ranking = jax.random.permutation(key, number_of)
    heavy_load, ordinary = portions_of(number_of, rows * top, most, skew, True), portions_of(number_of, rows * top, most, skew, False)
    places = jnp.arange(number_of)

    def named(sizes, rotation):
        used = int((sizes > 0).sum())
        fixed = max(1, used // 4)
        passed = fixed + (places - fixed + rotation * (used - fixed)) % max(1, number_of - fixed)
        return jnp.zeros((number_of,), jnp.int32).at[ranking[jnp.where(places < fixed, places, passed)]].set(jnp.asarray(sizes, jnp.int32))

    sizes = jnp.where(number % 4 == 0, named(heavy_load, number // 4), named(ordinary, number - number // 4 - 1))
    mixed = jax.random.permutation(jax.random.fold_in(own, 3), number_of)
    source_of, taker = mixed[0:number_of // 2 * 2:2], mixed[1:number_of // 2 * 2:2]
    slack = jnp.minimum(sizes[source_of] - 1, most - sizes[taker]) // 2
    slack = jnp.where((source_of == ranking[0]) | (taker == ranking[0]) | (sizes[taker] == 0), 0, jnp.maximum(slack, 0))
    passed = jax.random.randint(jax.random.fold_in(own, 4), (number_of // 2,), 0, 1 << 20) % (slack + 1)
    sizes = sizes.at[source_of].add(-passed).at[taker].add(passed)
    items = jnp.searchsorted(jnp.cumsum(sizes), jnp.arange(rows * top), side="right").astype(jnp.int32)
    listing = items.reshape(top, rows).T
    listing = listing[jax.random.permutation(jax.random.fold_in(own, 1), rows)]
    rotation = jax.random.randint(jax.random.fold_in(own, 2), (rows, 1), 0, top)
    return jnp.take_along_axis(listing, (jnp.arange(top)[None, :] + rotation) % top, axis=1)


def portions_of(count, total, limit, skew, full):
    loads = [(1 << 20) // math.isqrt(rank ** skew) + 1 for rank in range(1, count + 1)]
    largest = limit if full else min(limit, max(-(-total // count), total * loads[0] // sum(loads)))
    least = 1 if total - largest >= count - 1 else 0
    holding, spare = [largest] + [least] * (count - 1), total - largest - least * (count - 1)
    while spare > 0:
        movable = [i for i in range(1, count) if holding[i] < largest] or [i for i in range(1, count) if holding[i] < limit]
        whole, left = sum([loads[i] for i in movable]), spare
        for i in movable:
            extra = min(limit - holding[i], max(1, left * loads[i] // whole), spare)
            holding[i] = holding[i] + extra
            spare = spare - extra
    return np.array(holding)


def scatter_about(rng, shape, spread, most, cuts=(), kind=jnp.bfloat16):
    result = jax.random.normal(rng, shape, jnp.float32) * spread
    if len(cuts) > 0:
        result = block_levels(rng, shape, cuts, -0.22, 0.18) * result
    return jnp.clip(result, min=-most, max=most).astype(kind)


def setup_inputs(seed: int = 0) -> dict:
    streams_of = jax.random.split(jax.random.key(seed), 13)
    q_pre = draw_q_pre(jax.random.fold_in(streams_of[12], 71), 0)
    prefill_key_value = draw_prefill_key_value(jax.random.fold_in(streams_of[12], 71), 0)
    kv_past = draw_kv_past(jax.random.fold_in(streams_of[12], 71), 0)
    offset = jax.random.randint(streams_of[3], (1,), PREFIX_TOKENS // 2, PREFIX_TOKENS + 1).astype(jnp.int32)
    page_dest_keys = jax.random.split(jax.random.fold_in(streams_of[4], 1), STRETCH_PAGES // PAGES_DEV)
    page_dest_turns = jax.random.permutation(jax.random.fold_in(streams_of[4], 3), STRETCH_PAGES // PAGES_DEV)
    page_dest = jax.vmap(lambda own, number: deal_out(jax.random.fold_in(streams_of[4], 2), own, number, PAGES_DEV, N_CTX, 1, CAP, 2))(page_dest_keys, page_dest_turns).reshape((STRETCH_PAGES, 1))
    slot_perm = jax.vmap(lambda own: jax.random.permutation(own, POOL_SLOTS))(jax.random.split(streams_of[5], N_CTX)).reshape((N_CTX, POOL_SLOTS)).astype(jnp.int32)
    pool = draw_pool(jax.random.fold_in(streams_of[12], 71), 0)
    tables = touch_ends(jax.random.randint(streams_of[7], (DECODE_ROWS, ROW_PAGES), 0, POOL_SLOTS), jax.random.fold_in(streams_of[7], 1), 0, POOL_SLOTS - 1).astype(jnp.int32)
    lengths = jax.vmap(lambda own: ragged_sizes(own, INSTANCE_ROWS, INSTANCE_ROWS * ROW_PAGES * PAGE_TOKENS // 2, ROW_PAGES * PAGE_TOKENS, 2))(jax.random.split(streams_of[8], N_CTX)).reshape((N_CTX, INSTANCE_ROWS)).astype(jnp.int32)
    decode_query = draw_decode_query(jax.random.fold_in(streams_of[12], 71), 0)
    decode_key_value = scatter_about(streams_of[10], (2, DECODE_ROWS, DECODE_STEPS, KEY_VALUE_HEADS * HEAD_SIZE), 1.0, 4.0, ((1, 32), (3, 4)))
    out_weight = scatter_about(streams_of[11], (QUERY_HEADS * HEAD_SIZE, D), (QUERY_HEADS * HEAD_SIZE // 16) ** -0.5, 0.375, ((0, 4),))
    return dict(q_pre=q_pre, prefill_key_value=prefill_key_value, kv_past=kv_past, offset=offset, page_dest=page_dest, slot_perm=slot_perm, pool=pool, tables=tables, lengths=lengths, decode_query=decode_query, decode_key_value=decode_key_value, out_weight=out_weight)


def reference(q_pre, prefill_key_value, kv_past, offset, page_dest, slot_perm, pool, tables, lengths, decode_query, decode_key_value, out_weight):
    scaling = HEAD_SIZE ** -0.5
    query_groups = QUERY_HEADS // KEY_VALUE_HEADS
    all_keys = jnp.concatenate([kv_past[0], prefill_key_value[0]], axis=0)
    all_values = jnp.concatenate([kv_past[1], prefill_key_value[1]], axis=0)
    key_pos = jnp.arange(PREFIX_TOKENS + STRETCH_TOKENS, dtype=jnp.int32)
    q_block = math.gcd(STRETCH_TOKENS, 256)
    block_starts = jnp.arange(STRETCH_TOKENS // q_block, dtype=jnp.int32) * q_block

    def single_head(head_index):
        head_keys = lax.dynamic_slice_in_dim(all_keys, head_index * HEAD_SIZE, HEAD_SIZE, 1).astype(jnp.float32)
        head_values = lax.dynamic_slice_in_dim(all_values, head_index * HEAD_SIZE, HEAD_SIZE, 1).astype(jnp.float32)
        head_queries = lax.dynamic_slice_in_dim(q_pre, head_index * query_groups * HEAD_SIZE, query_groups * HEAD_SIZE, 1)

        def one_block(first_row):
            block_q = lax.dynamic_slice_in_dim(head_queries, first_row, q_block, 0).astype(jnp.float32).reshape(q_block, query_groups, HEAD_SIZE)
            query_pos = first_row + jnp.arange(q_block, dtype=jnp.int32)
            scores = jnp.einsum("qgh,kh->qgk", block_q, head_keys) * scaling
            allowed = jnp.where(key_pos[None, :] < PREFIX_TOKENS, key_pos[None, :] < offset[0], key_pos[None, :] - PREFIX_TOKENS <= query_pos[:, None])
            scores = jnp.where(allowed[:, None, :], scores, -jnp.inf)
            weights = jnp.exp(scores - jnp.max(scores, axis=-1, keepdims=True))
            totals = jnp.sum(weights, axis=-1)
            rounded = lax.optimization_barrier(weights.astype(jnp.bfloat16)).astype(jnp.float32)
            numerator = jnp.einsum("qgk,kh->qgh", rounded, head_values)
            return numerator / totals[..., None]

        return lax.map(one_block, block_starts)

    prefill_heads = lax.map(single_head, jnp.arange(KEY_VALUE_HEADS, dtype=jnp.int32))
    pre_out = jnp.transpose(prefill_heads, (1, 2, 0, 3, 4)).reshape(STRETCH_TOKENS, QUERY_HEADS * HEAD_SIZE).astype(jnp.bfloat16)

    target_slot = page_dest[:, 0]
    dest_hits = (target_slot[:, None] == jnp.arange(N_CTX, dtype=jnp.int32)[None, :]).astype(jnp.int32)
    page_rank = jnp.sum((jnp.cumsum(dest_hits, axis=0) - dest_hits) * dest_hits, axis=1).astype(jnp.int32)
    target_page_slot = slot_perm[target_slot, page_rank]
    stretch_page_view = prefill_key_value.reshape(2, STRETCH_PAGES, PAGE_TOKENS, KEY_VALUE_HEADS * HEAD_SIZE)
    pool_page_view = pool.reshape(2, N_CTX, POOL_SLOTS, PAGE_TOKENS, KEY_VALUE_HEADS * HEAD_SIZE).at[:, target_slot, target_page_slot].set(stretch_page_view)
    handed_pools = pool_page_view.reshape(2, N_CTX * POOL_SLOTS * PAGE_TOKENS, KEY_VALUE_HEADS * HEAD_SIZE)

    cached_extent = ROW_PAGES * PAGE_TOKENS
    causal = jnp.arange(DECODE_STEPS)[None, :] <= jnp.arange(DECODE_STEPS)[:, None]

    def one_instance(decode_instance):
        instance_pool = lax.dynamic_slice_in_dim(handed_pools, decode_instance * (POOL_SLOTS * PAGE_TOKENS), POOL_SLOTS * PAGE_TOKENS, 1)
        inst_tables = lax.dynamic_slice_in_dim(tables, decode_instance * INSTANCE_ROWS, INSTANCE_ROWS, 0)
        inst_lengths = lax.dynamic_slice_in_dim(lengths, decode_instance, 1, 0)[0]
        instance_queries = lax.dynamic_slice_in_dim(decode_query, decode_instance * INSTANCE_ROWS, INSTANCE_ROWS, 0).astype(jnp.float32).reshape(INSTANCE_ROWS, DECODE_STEPS, KEY_VALUE_HEADS, query_groups, HEAD_SIZE)
        instance_new_tokens = lax.dynamic_slice_in_dim(decode_key_value, decode_instance * INSTANCE_ROWS, INSTANCE_ROWS, 1).astype(jnp.float32).reshape(2, INSTANCE_ROWS, DECODE_STEPS, KEY_VALUE_HEADS, HEAD_SIZE)
        token_position = (inst_tables[:, :, None] * PAGE_TOKENS + jnp.arange(PAGE_TOKENS, dtype=jnp.int32)[None, None, :]).reshape(INSTANCE_ROWS, cached_extent)
        stored_keys = instance_pool[0][token_position].astype(jnp.float32).reshape(INSTANCE_ROWS, cached_extent, KEY_VALUE_HEADS, HEAD_SIZE)
        stored_values = instance_pool[1][token_position].astype(jnp.float32).reshape(INSTANCE_ROWS, cached_extent, KEY_VALUE_HEADS, HEAD_SIZE)
        live_cache = jnp.arange(cached_extent)[None, :] < inst_lengths[:, None]
        cache_scores = jnp.einsum("rtkgh,rckh->rtkgc", instance_queries, stored_keys) * scaling
        cache_scores = jnp.where(live_cache[:, None, None, None, :], cache_scores, -jnp.inf)
        fresh_scores = jnp.einsum("rtkgh,rskh->rtkgs", instance_queries, instance_new_tokens[0]) * scaling
        fresh_scores = jnp.where(causal[None, :, None, None, :], fresh_scores, -jnp.inf)
        row_max = jnp.maximum(jnp.max(cache_scores, axis=-1), jnp.max(fresh_scores, axis=-1))
        cache_weights = jnp.exp(cache_scores - row_max[..., None])
        fresh_weights = jnp.exp(fresh_scores - row_max[..., None])
        totals = jnp.sum(cache_weights, axis=-1) + jnp.sum(fresh_weights, axis=-1)
        cache_round = lax.optimization_barrier(cache_weights.astype(jnp.bfloat16)).astype(jnp.float32)
        fresh_round = lax.optimization_barrier(fresh_weights.astype(jnp.bfloat16)).astype(jnp.float32)
        numerator = jnp.einsum("rtkgc,rckh->rtkgh", cache_round, stored_values) + jnp.einsum("rtkgs,rskh->rtkgh", fresh_round, instance_new_tokens[1])
        return (numerator / totals[..., None]).astype(jnp.bfloat16).reshape(INSTANCE_ROWS, DECODE_STEPS, QUERY_HEADS * HEAD_SIZE)

    attn_dec = lax.map(one_instance, jnp.arange(N_CTX, dtype=jnp.int32)).reshape(DECODE_ROWS, DECODE_STEPS, QUERY_HEADS * HEAD_SIZE)
    dec_out = jnp.einsum("rtf,fd->rtd", attn_dec.astype(jnp.float32), out_weight.astype(jnp.float32)).astype(jnp.bfloat16)
    return (pre_out, handed_pools, dec_out)
```

```python
import functools

import jax
import jax.numpy as jnp
from jax import lax
from jax.experimental import pallas as pl
from jax.experimental.pallas import tpu as pltpu
from jax.sharding import PartitionSpec as P

HEAD = 128
PAGE = 16
N_CTX = 32
HEADS = 8
TOK = 256
HALF = 128
SCALE = (HEAD**-0.5) * 1.4426950408889634
NEG = -1e30
BLK = 1024
VMEM_BYTES = 56 * 2**20

RING_ORDER = (0, 3, 1, 2)


def shift_perm(axis, step):
    pairs = []
    for i in range(N_CTX):
        x, y, z = i // 16, (i // 4) % 4, i % 4
        if axis == "x":
            x = (x + step) % 2
        elif axis == "y":
            y = (y + step) % 4
        else:
            z = (z + step) % 4
        pairs.append((i, x * 16 + y * 4 + z))
    return pairs


def send(v, axis, step):
    return lax.ppermute(v, "ctx", shift_perm(axis, step))


def gather_pieces(piece, first, second):
    across = jnp.stack([piece, send(piece, "x", 1)])
    plus, minus = send(across, first, 1), send(across, first, -1)
    far_a, far_b = send(plus[0:1], first, 1), send(minus[1:2], first, -1)
    line = jnp.concatenate([across, plus, minus, far_a, far_b])
    up, down = send(line, second, 1), send(line, second, -1)
    up_far, down_far = send(up[:4], second, 1), send(down[4:], second, -1)
    held = [(dx, d) for d in RING_ORDER for dx in (0, 1)]

    def spec(entries, d2):
        out = []
        for dx, d1 in entries:
            out.append((dx, d1, d2) if first == "y" else (dx, d2, d1))
        return out

    arrays = [line, up, down, up_far, down_far]
    specs = [spec(held, 0), spec(held, 3), spec(held, 1), spec(held[:4], 2), spec(held[4:], 2)]
    return arrays, specs


def source_of(meta, dist):
    dx, dy, dz = dist
    return (meta[2] ^ dx) * 16 + ((meta[3] + dy) & 3) * 4 + ((meta[4] + dz) & 3)


def split_queries(q_ref, qs):
    for h in range(HEADS):
        scaled = q_ref[:, h * HEAD : (h + 1) * HEAD].astype(jnp.float32) * SCALE
        high = scaled.astype(jnp.bfloat16)
        qs[h * TOK : (h + 1) * TOK, 0:HEAD] = high
        qs[h * TOK : (h + 1) * TOK, HEAD:] = (scaled - high.astype(jnp.float32)).astype(jnp.bfloat16)


def fold(qs, m_s, acc_s, k, v, mask):
    k2 = jnp.concatenate([k, k], axis=1)
    v2 = jnp.concatenate([v, jnp.ones_like(v)], axis=1)

    def score(h):
        s = lax.dot_general(
            qs[h * TOK : (h + 1) * TOK, :], k2, (((1,), (1,)), ((), ())), preferred_element_type=jnp.float32
        )
        return s if mask is None else jnp.where(mask, s, NEG)

    def soft(h, s):
        rows = slice(h * TOK, (h + 1) * TOK)
        old = m_s[rows, :]
        new = jnp.maximum(old, jnp.max(s, axis=1, keepdims=True))
        m_s[rows, :] = new
        return jnp.exp2(s - new[:, 0:1]).astype(jnp.bfloat16), jnp.exp2(old - new)

    def add(h, p, a):
        rows = slice(h * TOK, (h + 1) * TOK)
        acc_s[rows, :] = acc_s[rows, :] * jnp.concatenate([a, a], axis=1) + jnp.dot(
            p, v2, preferred_element_type=jnp.float32
        )

    scores, weights = {}, {}
    for t in range(HEADS + 2):
        if t < HEADS:
            scores[t] = score(t)
        if 0 <= t - 1 < HEADS:
            weights[t - 1] = soft(t - 1, scores.pop(t - 1))
        if 0 <= t - 2 < HEADS:
            add(t - 2, *weights.pop(t - 2))


def flash_kernel(specs, halves, past, own, has_state, last, n_dep, *refs):
    refs = list(refs)
    meta, q_ref = refs[0], refs[1]
    refs = refs[2:]
    arrays, refs = refs[: len(specs)], refs[len(specs) :]
    if own:
        own_kv, own_past, refs = refs[0], refs[1], refs[2:]
    if has_state:
        acc_in, ml_in, refs = refs[0], refs[1], refs[2:]
    refs = refs[n_dep:]
    outs, refs = refs[: 1 if last else 2], refs[1 if last else 2 :]
    k_s, v_s, qs, m_s, acc_s, sems = refs

    me, offset = meta[0], meta[1]
    todo = []
    full = jnp.int32(0)
    part_len = jnp.int32(0)
    for array, spec, half in zip(arrays, specs, halves):
        for j, dist in enumerate(spec):
            if dist == (0, 0, 0):
                continue
            src = source_of(meta, dist)
            if past:
                length = jnp.clip(offset - src * TOK - half * HALF, 0, HALF)
            else:
                length = jnp.where(src < me, HALF, 0)
            todo.append((array, j, length))
    for array, j, length in todo:
        full = full + (length == HALF).astype(jnp.int32)
    tail_at = full
    at = jnp.int32(0)
    copies = []
    for n, (array, j, length) in enumerate(todo):
        is_full = length == HALF
        row = pl.multiple_of(jnp.where(is_full, at, tail_at) * HALF, HALF)
        at = at + is_full.astype(jnp.int32)
        part_len = part_len + jnp.where(is_full, 0, length)
        kc = pltpu.make_async_copy(array.at[j, pl.ds(0, HALF)], k_s.at[pl.ds(row, HALF)], sems.at[2 * n])
        vc = pltpu.make_async_copy(array.at[j, pl.ds(HALF, HALF)], v_s.at[pl.ds(row, HALF)], sems.at[2 * n + 1])
        copies.append((length > 0, kc, vc))

        @pl.when(length > 0)
        def _():
            kc.start()
            vc.start()

    count = full * HALF + part_len

    split_queries(q_ref, qs)
    if has_state:
        lane = lax.broadcasted_iota(jnp.int32, (TOK, HEAD), 1)
        packed = ml_in[...]
        for h in range(HEADS):
            rows = slice(h * TOK, (h + 1) * TOK)
            m_s[rows, :] = jnp.broadcast_to(
                jnp.sum(jnp.where(lane == h, packed, 0.0), axis=1, keepdims=True), (TOK, HEAD)
            )
            acc_s[rows, 0:HEAD] = acc_in[rows, :]
            acc_s[rows, HEAD:] = jnp.broadcast_to(
                jnp.sum(jnp.where(lane == HEADS + h, packed, 0.0), axis=1, keepdims=True), (TOK, HEAD)
            )
    else:
        m_s[...] = jnp.full_like(m_s, NEG)
        acc_s[...] = jnp.zeros_like(acc_s)

    if own:
        row = lax.broadcasted_iota(jnp.int32, (TOK, 2 * TOK), 0)
        col = lax.broadcasted_iota(jnp.int32, (TOK, 2 * TOK), 1)
        mask = (col <= row) | ((col >= TOK) & (col - TOK + me * TOK < offset))
        fold(
            qs,
            m_s,
            acc_s,
            jnp.concatenate([own_kv[0], own_past[0]], axis=0),
            jnp.concatenate([own_kv[1], own_past[1]], axis=0),
            mask,
        )

    for live, kc, vc in copies:

        @pl.when(live)
        def _():
            kc.wait()
            vc.wait()

    if copies:
        whole = count // BLK

        def step(i, _):
            at = pl.multiple_of(i * BLK, BLK)
            fold(qs, m_s, acc_s, k_s[pl.ds(at, BLK), :], v_s[pl.ds(at, BLK), :], None)
            return 0

        lax.fori_loop(0, whole, step, 0)
        left = count - whole * BLK

        @pl.when(left > 0)
        def _():
            at = pl.multiple_of(whole * BLK, BLK)
            col = lax.broadcasted_iota(jnp.int32, (TOK, BLK), 1)
            vrow = lax.broadcasted_iota(jnp.int32, (BLK, HEAD), 0)
            v = v_s[pl.ds(at, BLK), :]
            v = jnp.where(vrow < left, v.astype(jnp.float32), 0.0).astype(jnp.bfloat16)
            fold(qs, m_s, acc_s, k_s[pl.ds(at, BLK), :], v, col < left)

    if last:
        for h in range(HEADS):
            rows = slice(h * TOK, (h + 1) * TOK)
            outs[0][:, h * HEAD : (h + 1) * HEAD] = (acc_s[rows, 0:HEAD] / acc_s[rows, HEAD:]).astype(jnp.bfloat16)
    else:
        lane = lax.broadcasted_iota(jnp.int32, (TOK, HEAD), 1)
        packed = jnp.zeros((TOK, HEAD), jnp.float32)
        for h in range(HEADS):
            rows = slice(h * TOK, (h + 1) * TOK)
            packed = jnp.where(lane == h, m_s[rows, :], packed)
            packed = jnp.where(lane == HEADS + h, acc_s[rows, HEAD:], packed)
            outs[0][rows, :] = acc_s[rows, 0:HEAD]
        outs[1][...] = packed


def flash(meta, q, gathered, past, own=None, state=None, last=False, deps=(), units=16, name="flash"):
    smem = pl.BlockSpec(memory_space=pltpu.SMEM)
    vmem = pl.BlockSpec(memory_space=pltpu.VMEM)
    any_ = pl.BlockSpec(memory_space=pl.ANY)
    args, specs_in = [meta, q], [smem, vmem]
    for array, _, _ in gathered:
        args.append(array)
        specs_in.append(any_)
    for group in (own, state):
        if group is not None:
            args += list(group)
            specs_in += [vmem, vmem]
    args += list(deps)
    specs_in += [any_] * len(deps)
    pieces = sum(len(s) for _, s, _ in gathered)
    rows = max(BLK, -(-pieces * HALF // BLK) * BLK)
    if last:
        out_shape = jax.ShapeDtypeStruct((TOK, HEADS * HEAD), jnp.bfloat16)
        out_specs = vmem
    else:
        out_shape = (
            jax.ShapeDtypeStruct((HEADS * TOK, HEAD), jnp.float32),
            jax.ShapeDtypeStruct((TOK, HEAD), jnp.float32),
        )
        out_specs = (vmem, vmem)
    work = units * TOK * TOK * HEADS
    return pl.pallas_call(
        functools.partial(
            flash_kernel,
            [s for _, s, _ in gathered],
            [h for _, _, h in gathered],
            past,
            own is not None,
            state is not None,
            last,
            len(deps),
        ),
        out_shape=out_shape,
        in_specs=specs_in,
        out_specs=out_specs,
        scratch_shapes=[
            pltpu.VMEM((rows, HEAD), jnp.bfloat16),
            pltpu.VMEM((rows, HEAD), jnp.bfloat16),
            pltpu.VMEM((HEADS * TOK, 2 * HEAD), jnp.bfloat16),
            pltpu.VMEM((HEADS * TOK, HEAD), jnp.float32),
            pltpu.VMEM((HEADS * TOK, 2 * HEAD), jnp.float32),
            pltpu.SemaphoreType.DMA((2 * max(pieces, 1),)),
        ],
        compiler_params=pltpu.CompilerParams(vmem_limit_bytes=VMEM_BYTES),
        cost_estimate=pl.CostEstimate(flops=work * HEAD * 8, bytes_accessed=pieces * 65536, transcendentals=work),
        name=name,
    )(*args)


def decode_kernel(specs, halves, *refs):
    refs = list(refs)
    meta, dest, perm, table, length, q_ref, fresh, pool = refs[:8]
    refs = refs[8:]
    arrays, refs = refs[: len(specs)], refs[len(specs) :]
    attn, pool_out, refs = refs[0], refs[1], refs[2:]
    k_s, v_s, qs, bias, arrivals, sems = refs
    me = meta[0]

    copies = []
    n = 0
    for array, spec, half in zip(arrays, specs, halves):
        for j, dist in enumerate(spec):
            row = pl.multiple_of(source_of(meta, dist) * TOK + half * HALF, HALF)
            kc = pltpu.make_async_copy(array.at[j, pl.ds(0, HALF)], k_s.at[pl.ds(row, HALF)], sems.at[2 * n])
            vc = pltpu.make_async_copy(array.at[j, pl.ds(HALF, HALF)], v_s.at[pl.ds(row, HALF)], sems.at[2 * n + 1])
            kc.start()
            vc.start()
            copies += [kc, vc]
            n += 1

    def scan_chunk(c, found):
        dx = (c >> 4) ^ meta[2]
        dy = ((c >> 2) - meta[3]) & 3
        dz = (c - meta[4]) & 3
        place = lambda d: jnp.where(d == 0, 0, jnp.where(d == 3, 1, jnp.where(d == 1, 2, 3)))
        base = (place(dz) * 8 + place(dy) * 2 + dx) * PAGE
        for i in range(PAGE):
            arrivals[found] = c * PAGE + i
            found = found + (dest[base + i] == me).astype(jnp.int32)
        return found

    found = lax.fori_loop(0, N_CTX, scan_chunk, jnp.int32(0))

    rows = table.shape[0]
    slots = perm.shape[0]
    slot_id = lax.broadcasted_iota(jnp.int32, (rows, slots), 1)
    live = length[...]
    whole = live >> 4
    times = jnp.zeros((rows, slots), jnp.float32)
    ending = jnp.zeros((rows, slots), jnp.float32)
    for a in range(table.shape[1]):
        hit = table[:, a : a + 1] == slot_id
        times = times + jnp.where(hit & (whole > a), 1.0, 0.0)
        ending = ending + jnp.where(hit & (whole == a), 1.0, 0.0)
    tokens = pool.shape[1]
    spread = (
        lax.broadcasted_iota(jnp.int32, (slots, tokens), 1) // PAGE
        == lax.broadcasted_iota(jnp.int32, (slots, tokens), 0)
    )
    spread = jnp.where(spread, 1.0, 0.0).astype(jnp.bfloat16)
    in_page = lax.broadcasted_iota(jnp.int32, (rows, tokens), 1) % PAGE
    times = jnp.dot(times.astype(jnp.bfloat16), spread, preferred_element_type=jnp.float32)
    ending = jnp.dot(ending.astype(jnp.bfloat16), spread, preferred_element_type=jnp.float32)
    times = times + jnp.where(in_page < (live & 15), ending, 0.0)
    bias[:, 0:tokens] = jnp.where(times > 0.5, jnp.log2(jnp.maximum(times, 1.0)), NEG)
    r = lax.broadcasted_iota(jnp.int32, (rows, rows), 0)
    c = lax.broadcasted_iota(jnp.int32, (rows, rows), 1)
    bias[:, tokens:] = jnp.where(((r >> 2) == (c >> 2)) & (c <= r), 0.0, NEG)

    split_queries(q_ref, qs)
    pool_out[...] = pool[...]
    for copy in copies:
        copy.wait()

    def place_page(i, _):
        src = pl.multiple_of(arrivals[i] * PAGE, PAGE)
        dst = pl.multiple_of(perm[i] * PAGE, PAGE)
        pool_out[0, pl.ds(dst, PAGE), :] = k_s[pl.ds(src, PAGE), :]
        pool_out[1, pl.ds(dst, PAGE), :] = v_s[pl.ds(src, PAGE), :]
        return 0

    lax.fori_loop(0, found, place_page, 0)

    k = jnp.concatenate([pool_out[0], fresh[0]], axis=0)
    v = jnp.concatenate([pool_out[1], fresh[1]], axis=0)
    k2 = jnp.concatenate([k, k], axis=1)
    v2 = jnp.concatenate([v, jnp.ones_like(v)], axis=1)
    scores, weights = {}, {}
    for t in range(HEADS + 2):
        if t < HEADS:
            scores[t] = lax.dot_general(
                qs[t * TOK : (t + 1) * TOK, :], k2, (((1,), (1,)), ((), ())), preferred_element_type=jnp.float32
            )
        if 0 <= t - 1 < HEADS:
            s = scores.pop(t - 1) + bias[...]
            weights[t - 1] = jnp.exp2(s - jnp.max(s, axis=1, keepdims=True)).astype(jnp.bfloat16)
        if 0 <= t - 2 < HEADS:
            out = jnp.dot(weights.pop(t - 2), v2, preferred_element_type=jnp.float32)
            attn[:, (t - 2) * HEAD : (t - 1) * HEAD] = (out[:, 0:HEAD] / out[:, HEAD:]).astype(jnp.bfloat16)


def decode(meta, dest, perm, table, length, q, fresh, pool, gathered):
    smem = pl.BlockSpec(memory_space=pltpu.SMEM)
    vmem = pl.BlockSpec(memory_space=pltpu.VMEM)
    any_ = pl.BlockSpec(memory_space=pl.ANY)
    rows = q.shape[0]
    keys = pool.shape[1] + rows
    return pl.pallas_call(
        functools.partial(decode_kernel, [s for _, s, _ in gathered], [h for _, _, h in gathered]),
        out_shape=(
            jax.ShapeDtypeStruct(q.shape, jnp.bfloat16),
            jax.ShapeDtypeStruct(pool.shape, jnp.bfloat16),
        ),
        in_specs=[smem, smem, smem] + [vmem] * 5 + [any_] * len(gathered),
        out_specs=(vmem, vmem),
        scratch_shapes=[
            pltpu.VMEM((N_CTX * TOK, HEAD), jnp.bfloat16),
            pltpu.VMEM((N_CTX * TOK, HEAD), jnp.bfloat16),
            pltpu.VMEM((HEADS * rows, 2 * HEAD), jnp.bfloat16),
            pltpu.VMEM((rows, keys), jnp.float32),
            pltpu.SMEM((N_CTX * PAGE + 8,), jnp.int32),
            pltpu.SemaphoreType.DMA((4 * N_CTX,)),
        ],
        compiler_params=pltpu.CompilerParams(vmem_limit_bytes=VMEM_BYTES),
        cost_estimate=pl.CostEstimate(
            flops=HEADS * rows * keys * HEAD * 8, bytes_accessed=6 * 2**20, transcendentals=HEADS * rows * keys
        ),
        name="decode",
    )(meta, dest, perm, table, length, q, fresh, pool, *[a for a, _, _ in gathered])


def project_kernel(a_ref, w_ref, o_ref):
    o_ref[...] = jnp.dot(a_ref[...], w_ref[...], preferred_element_type=jnp.float32).astype(jnp.bfloat16)


def project(attn, weight, start, width, tile=512):
    rows, depth = attn.shape
    first = start // tile
    return pl.pallas_call(
        project_kernel,
        grid=(width // tile,),
        out_shape=jax.ShapeDtypeStruct((rows, width), jnp.bfloat16),
        in_specs=[
            pl.BlockSpec((rows, depth), lambda i: (0, 0)),
            pl.BlockSpec((depth, tile), lambda i: (0, first + i)),
        ],
        out_specs=pl.BlockSpec((rows, tile), lambda i: (0, i)),
        compiler_params=pltpu.CompilerParams(vmem_limit_bytes=VMEM_BYTES),
        cost_estimate=pl.CostEstimate(
            flops=2 * rows * depth * width, bytes_accessed=2 * depth * width, transcendentals=0
        ),
        name="project",
    )(attn, weight)


def body(
    q_pre,
    prefill_key_value,
    kv_past,
    offset,
    page_dest,
    slot_perm,
    pool,
    tables,
    lengths,
    decode_query,
    decode_key_value,
    out_weight,
):
    me = lax.axis_index("ctx").astype(jnp.int32)
    tp = lax.axis_index("tp").astype(jnp.int32)
    meta = jnp.stack([me, offset[0], me // 16, (me // 4) % 4, me % 4, jnp.int32(0), jnp.int32(0), jnp.int32(0)])

    dest_rows = jnp.broadcast_to(page_dest.astype(jnp.bfloat16), (PAGE, HEAD))
    kv = prefill_key_value
    near_a = jnp.concatenate([kv[0, :HALF], kv[1, :HALF], dest_rows])
    near_b = jnp.concatenate([kv[0, HALF:], kv[1, HALF:]])
    arrays_a, specs_a = gather_pieces(near_a, "y", "z")
    arrays_b, specs_b = gather_pieces(near_b, "z", "y")
    stretch = [(a, s, 0) for a, s in zip(arrays_a, specs_a)] + [(a, s, 1) for a, s in zip(arrays_b, specs_b)]

    state = flash(meta, q_pre, [], False, own=(kv, kv_past), units=2, name="flash_own")

    dest = jnp.concatenate([a[:, 2 * HALF :, 0] for a in arrays_a]).astype(jnp.int32).reshape(-1)
    rows_dev, steps = decode_query.shape[0], decode_query.shape[1]
    rows = rows_dev * steps
    attn, new_pool = decode(
        meta,
        dest,
        slot_perm[0],
        jnp.repeat(tables, steps, axis=0),
        jnp.repeat(lengths.reshape(rows_dev, 1), steps, axis=0),
        decode_query.reshape(rows, -1),
        decode_key_value.reshape(2, rows, HEAD),
        pool,
        stretch,
    )

    past = kv_past
    past_a, pspecs_a = gather_pieces(jnp.concatenate([past[0, :HALF], past[1, :HALF]]), "y", "z")
    past_b, pspecs_b = gather_pieces(jnp.concatenate([past[0, HALF:], past[1, HALF:]]), "z", "y")
    cached = [(a, s, 0) for a, s in zip(past_a, pspecs_a)] + [(a, s, 1) for a, s in zip(past_b, pspecs_b)]

    width = out_weight.shape[1]
    part = width // 4
    share = rows // 4
    core, far = tp % 2, tp // 2
    core_perm = [(0, 1), (1, 0), (2, 3), (3, 2)]
    far_perm = [(0, 2), (1, 3), (2, 0), (3, 1)]
    results = []
    dep = None
    for c in range(4):
        term = project(attn, out_weight, c * part, part).reshape(2, 2, share, part)
        dep = term
        mine = lax.dynamic_index_in_dim(term, core, 1, keepdims=False)
        theirs = lax.dynamic_index_in_dim(term, 1 - core, 1, keepdims=False)
        got = lax.ppermute(theirs, "tp", core_perm)
        both = (mine.astype(jnp.float32) + got.astype(jnp.float32)).astype(jnp.bfloat16)
        keep = lax.dynamic_index_in_dim(both, far, 0, keepdims=False)
        away = lax.dynamic_index_in_dim(both, 1 - far, 0, keepdims=False)
        got = lax.ppermute(away, "tp", far_perm)
        results.append((keep.astype(jnp.float32) + got.astype(jnp.float32)).astype(jnp.bfloat16))
    dec_out = jnp.concatenate(results, axis=1).reshape(share // steps, steps, width)

    state = flash(meta, q_pre, stretch, False, state=state, units=31, deps=(dep,), name="flash_stretch")
    pre_out = flash(meta, q_pre, cached, True, state=state, last=True, units=31, name="flash_past")
    return (pre_out, new_pool, dec_out)


def solution(mesh):
    return jax.shard_map(
        body,
        mesh=mesh,
        in_specs=(
            P("ctx", "tp"),
            P(None, "ctx", "tp"),
            P(None, "ctx", "tp"),
            P(),
            P("ctx", None),
            P("ctx", None),
            P(None, "ctx", "tp"),
            P("ctx", None),
            P("ctx", None),
            P("ctx", None, "tp"),
            P(None, "ctx", None, "tp"),
            P("tp", None),
        ),
        out_specs=(P("ctx", "tp"), P(None, "ctx", "tp"), P(("ctx", "tp"), None, None)),
        check_vma=False,
    )
```

```python
import functools

import jax
import jax.numpy as jnp
from jax import lax
from jax.experimental import pallas as pl
from jax.experimental.pallas import tpu as pltpu
from jax.sharding import PartitionSpec as P

HEAD = 128
PAGE = 16
CAP = 2
N_CTX = 32
HEADS = 8
POOL_SLOTS = 64
TOK = 256
CHUNKS = 8
SCALE = (HEAD**-0.5) * 1.4426950408889634
NEG = -1e30
BIG = 2048
SMALL = 1024
VMEM_BYTES = 56 * 2**20

SMEM = pl.BlockSpec(memory_space=pltpu.SMEM)
VMEM = pl.BlockSpec(memory_space=pltpu.VMEM)
ANY = pl.BlockSpec(memory_space=pl.ANY)


def shift_perm(axis, step):
    pairs = []
    for i in range(N_CTX):
        x, y, z = i // 16, (i // 4) % 4, i % 4
        if axis == "x":
            x = (x + step) % 2
        elif axis == "y":
            y = (y + step) % 4
        else:
            z = (z + step) % 4
        pairs.append((i, x * 16 + y * 4 + z))
    return pairs


def send(v, axis, step):
    return lax.ppermute(v, "ctx", shift_perm(axis, step))


def iota(shape, dim):
    return lax.broadcasted_iota(jnp.int32, shape, dim)


def hot(mask):
    return jnp.where(mask, 1.0, 0.0).astype(jnp.bfloat16)


def dot(a, b):
    return jnp.dot(a, b, preferred_element_type=jnp.float32)


def prep_kernel(kv, past, dest_row, out, pack):
    pack[0] = kv[...]
    pack[1] = past[...]
    pages = dest_row.shape[1]
    hits = jnp.where(iota((N_CTX, pages), 0) == dest_row[...], 1.0, 0.0)
    before = hot(iota((pages, pages), 0) < iota((pages, pages), 1))
    rank = jnp.sum(hits * dot(hits.astype(jnp.bfloat16), before), axis=0, keepdims=True)
    key = dest_row[...].astype(jnp.float32) * CAP + rank
    key = jnp.broadcast_to(key, (8, pages)).astype(jnp.bfloat16)
    tokens = pages * PAGE
    spread = hot(iota((pages, tokens), 1) // PAGE == iota((pages, tokens), 0))
    target = dot(key, spread)[0:1, :] * PAGE + (iota((1, tokens), 1) % PAGE).astype(jnp.float32)
    rows = N_CTX * CAP * PAGE
    pick = hot(iota((rows, tokens), 0).astype(jnp.float32) == target)
    both = dot(pick, jnp.concatenate([kv[0], kv[1]], axis=1)).astype(jnp.bfloat16)
    out[:, 0 : CAP * PAGE, :] = both[:, 0:HEAD].reshape(N_CTX, CAP * PAGE, HEAD)
    out[:, CAP * PAGE : 2 * CAP * PAGE, :] = both[:, HEAD:].reshape(N_CTX, CAP * PAGE, HEAD)
    count = jnp.broadcast_to(jnp.sum(hits, axis=1, keepdims=True), (N_CTX, HEAD)).astype(jnp.bfloat16)
    repeat = hot(iota((N_CTX * PAGE, N_CTX), 0) // PAGE == iota((N_CTX * PAGE, N_CTX), 1))
    out[:, 2 * CAP * PAGE :, :] = dot(repeat, count).astype(jnp.bfloat16).reshape(N_CTX, PAGE, HEAD)


def prep(kv, past, page_dest):
    return pl.pallas_call(
        prep_kernel,
        out_shape=(
            jax.ShapeDtypeStruct((N_CTX, (2 * CAP + 1) * PAGE, HEAD), jnp.bfloat16),
            jax.ShapeDtypeStruct((2,) + kv.shape, jnp.bfloat16),
        ),
        in_specs=[VMEM] * 3,
        out_specs=(VMEM, VMEM),
        compiler_params=pltpu.CompilerParams(vmem_limit_bytes=VMEM_BYTES),
        name="prep",
    )(kv, past, page_dest.reshape(1, -1))


def split_queries(q_ref, qs):
    for h in range(HEADS):
        scaled = q_ref[:, h * HEAD : (h + 1) * HEAD].astype(jnp.float32) * SCALE
        high = scaled.astype(jnp.bfloat16)
        qs[h * TOK : (h + 1) * TOK, 0:HEAD] = high
        qs[h * TOK : (h + 1) * TOK, HEAD:] = (scaled - high.astype(jnp.float32)).astype(jnp.bfloat16)


def fold(qs, m_s, acc_s, k, v, mask=None, ones=None):
    k2 = jnp.concatenate([k, k], axis=1)
    v2 = jnp.concatenate([v, jnp.ones_like(v) if ones is None else ones], axis=1)

    def score(h):
        s = lax.dot_general(
            qs[h * TOK : (h + 1) * TOK, :], k2, (((1,), (1,)), ((), ())), preferred_element_type=jnp.float32
        )
        return s if mask is None else jnp.where(mask, s, NEG)

    def soft(h, s):
        rows = slice(h * TOK, (h + 1) * TOK)
        old = m_s[rows, :]
        new = jnp.maximum(old, jnp.max(s, axis=1, keepdims=True))
        m_s[rows, :] = new
        return jnp.exp2(s - new[:, 0:1]).astype(jnp.bfloat16), jnp.exp2(old - new)

    def add(h, p, a):
        rows = slice(h * TOK, (h + 1) * TOK)
        acc_s[rows, :] = acc_s[rows, :] * jnp.concatenate([a, a], axis=1) + dot(p, v2)

    scores, weights = {}, {}
    for t in range(HEADS + 2):
        if t < HEADS:
            scores[t] = score(t)
        if 0 <= t - 1 < HEADS:
            weights[t - 1] = soft(t - 1, scores.pop(t - 1))
        if 0 <= t - 2 < HEADS:
            add(t - 2, *weights.pop(t - 2))


def flash_kernel(dz, n_dep, offset_ref, q_ref, near, plus, minus, far, *refs):
    out, k_s, v_s, ones_s, qs, m_s, acc_s, sems = refs[n_dep:]
    me, offset = lax.axis_index("ctx"), offset_ref[0]
    x, y, z = me >> 4, (me >> 2) & 3, me & 3
    group = me >> 2
    zq = (z + dz) & 3
    seen = group + (z < zq).astype(jnp.int32)
    count = seen * TOK
    copies = []
    for s in range(2):
        for array, dy in ((near, 0), (plus, 3), (minus, 1), (far, 2)):
            for dx in range(2):
                j = (x ^ dx) * 4 + ((y + dy) & 3)
                if s == 0:
                    live = j < seen
                    row = j * TOK
                else:
                    length = jnp.clip(offset - (j * 4 + z) * TOK, 0, TOK)
                    live = length > 0
                    row = (seen + j) * TOK
                    count = count + length
                row = pl.multiple_of(row, TOK)
                n = len(copies)
                kc = pltpu.make_async_copy(array.at[dx, s, 0], k_s.at[pl.ds(row, TOK)], sems.at[2 * n])
                vc = pltpu.make_async_copy(array.at[dx, s, 1], v_s.at[pl.ds(row, TOK)], sems.at[2 * n + 1])
                copies.append((live, kc, vc))

                @pl.when(live)
                def _():
                    kc.start()
                    vc.start()

    split_queries(q_ref, qs)
    m_s[...] = jnp.full_like(m_s, NEG)
    acc_s[...] = jnp.zeros_like(acc_s)

    if dz == 0:
        own_k = pltpu.make_async_copy(near.at[0, 0, 0], k_s.at[pl.ds(2 * CHUNKS * TOK, TOK)], sems.at[64])
        own_v = pltpu.make_async_copy(near.at[0, 0, 1], v_s.at[pl.ds(2 * CHUNKS * TOK, TOK)], sems.at[65])
        own_k.start()
        own_v.start()
        own_k.wait()
        own_v.wait()
        mask = iota((TOK, TOK), 1) <= iota((TOK, TOK), 0)
        fold(qs, m_s, acc_s, k_s[2 * CHUNKS * TOK :, :], v_s[2 * CHUNKS * TOK :, :], mask)

    for live, kc, vc in copies:

        @pl.when(live)
        def _():
            kc.wait()
            vc.wait()

    last = (count - 1) // BIG
    left = count - last * BIG
    end = pl.multiple_of(last * BIG, BIG)
    for at in range(0, BIG, 512):
        inside = iota((512, HEAD), 0) + at < left
        rows = pl.ds(pl.multiple_of(end + at, 512), 512)
        first = k_s[pl.ds(end, 16), :][0:1, :].astype(jnp.float32)
        k_s[rows, :] = jnp.where(inside, k_s[rows, :].astype(jnp.float32), first).astype(jnp.bfloat16)
        v_s[rows, :] = jnp.where(inside, v_s[rows, :].astype(jnp.float32), 0.0).astype(jnp.bfloat16)
        ones_s[at : at + 512, :] = jnp.where(inside, 1.0, 0.0).astype(jnp.bfloat16)

    def block(at, size, ones):
        fold(qs, m_s, acc_s, k_s[pl.ds(at, size), :], v_s[pl.ds(at, size), :], None, ones)

    def step(i, _):
        ones = jnp.maximum(ones_s[...], jnp.where(i < last, 1.0, 0.0).astype(jnp.bfloat16))
        block(pl.multiple_of(i * BIG, BIG), BIG, ones)
        return 0

    lax.fori_loop(0, last + (left > SMALL).astype(jnp.int32), step, 0)

    @pl.when(left <= SMALL)
    def _():
        block(end, SMALL, ones_s[0:SMALL, :])

    lane = iota((TOK, HEAD), 1)
    level = jnp.zeros((TOK, HEAD), jnp.float32)
    for h in range(HEADS):
        rows = slice(h * TOK, (h + 1) * TOK)
        total = acc_s[rows, HEAD:]
        out[:, h * HEAD : (h + 1) * HEAD] = (acc_s[rows, 0:HEAD] / total).astype(jnp.bfloat16)
        value = m_s[rows, :] + jnp.log2(total)
        high = value.astype(jnp.bfloat16).astype(jnp.float32)
        middle = (value - high).astype(jnp.bfloat16).astype(jnp.float32)
        low = value - high - middle
        level = jnp.where(lane == h, high, level)
        level = jnp.where(lane == HEADS + h, middle, level)
        level = jnp.where(lane == 2 * HEADS + h, low, level)
    out[:, HEADS * HEAD :] = level.astype(jnp.bfloat16)


def flash(offset, q, arrays, dz, deps=()):
    work = 2 * CHUNKS * TOK * TOK * HEADS
    rows = (2 * CHUNKS + 1) * TOK
    return pl.pallas_call(
        functools.partial(flash_kernel, dz, len(deps)),
        out_shape=jax.ShapeDtypeStruct((TOK, HEADS * HEAD + HEAD), jnp.bfloat16),
        in_specs=[SMEM, VMEM] + [ANY] * (4 + len(deps)),
        out_specs=VMEM,
        scratch_shapes=[
            pltpu.VMEM((rows, HEAD), jnp.bfloat16),
            pltpu.VMEM((rows, HEAD), jnp.bfloat16),
            pltpu.VMEM((BIG, HEAD), jnp.bfloat16),
            pltpu.VMEM((HEADS * TOK, 2 * HEAD), jnp.bfloat16),
            pltpu.VMEM((HEADS * TOK, HEAD), jnp.float32),
            pltpu.VMEM((HEADS * TOK, 2 * HEAD), jnp.float32),
            pltpu.SemaphoreType.DMA((66,)),
        ],
        compiler_params=pltpu.CompilerParams(vmem_limit_bytes=VMEM_BYTES),
        cost_estimate=pl.CostEstimate(flops=work * HEAD * 8, bytes_accessed=3 * 2**20, transcendentals=work),
        name=f"flash{dz}",
    )(offset, q, *arrays, *deps)


def combine_kernel(*refs):
    parts, out = refs[:-1], refs[-1]
    width = HEADS * HEAD
    levels = []
    for part in parts:
        three = part[:, width:].astype(jnp.float32)
        levels.append(three[:, 0:HEADS] + three[:, HEADS : 2 * HEADS] + three[:, 2 * HEADS : 3 * HEADS])
    top = functools.reduce(jnp.maximum, levels)
    shares = [jnp.exp2(v - top) for v in levels]
    total = functools.reduce(jnp.add, shares)
    shares = [s / total for s in shares]
    for h in range(HEADS):
        cols = slice(h * HEAD, (h + 1) * HEAD)
        acc = jnp.zeros((TOK, HEAD), jnp.float32)
        for part, share in zip(parts, shares):
            acc = acc + part[:, cols].astype(jnp.float32) * share[:, h : h + 1]
        out[:, cols] = acc.astype(jnp.bfloat16)


def combine(parts):
    return pl.pallas_call(
        combine_kernel,
        out_shape=jax.ShapeDtypeStruct((TOK, HEADS * HEAD), jnp.bfloat16),
        in_specs=[VMEM] * len(parts),
        out_specs=VMEM,
        compiler_params=pltpu.CompilerParams(vmem_limit_bytes=VMEM_BYTES),
        name="combine",
    )(*parts)


TILES = 4


def bias_kernel(table, length, out):
    pages, rows = table.shape
    slots, steps = POOL_SLOTS, out.shape[0] // rows
    tokens, all_rows = slots * PAGE, rows * steps
    live = length[...]
    whole = live >> 4
    slot_id = iota((slots, rows), 0)
    times = jnp.zeros((slots, rows), jnp.float32)
    ending = jnp.zeros((slots, rows), jnp.float32)
    for a in range(pages):
        hit = table[a : a + 1, :] == slot_id
        times = times + jnp.where(hit & (whole > a), 1.0, 0.0)
        ending = ending + jnp.where(hit & (whole == a), 1.0, 0.0)
    repeat = hot(iota((rows, all_rows), 0) == iota((rows, all_rows), 1) // steps)
    spread = hot(iota((slots, tokens), 1) // PAGE == iota((slots, tokens), 0))
    rest = jnp.broadcast_to((live & 15).astype(jnp.float32), (8, rows)).astype(jnp.bfloat16)
    rest = dot(rest, repeat)[0:1, :]
    r, c = iota((all_rows, all_rows), 0), iota((all_rows, all_rows), 1)
    rest = jnp.sum(jnp.where(r == c, rest, 0.0), axis=1, keepdims=True)

    def widen(v):
        v = dot(v.astype(jnp.bfloat16), repeat).astype(jnp.bfloat16)
        return lax.dot_general(v, spread, (((0,), (0,)), ((), ())), preferred_element_type=jnp.float32)

    in_page = (iota((all_rows, tokens), 1) % PAGE).astype(jnp.float32)
    count = widen(times) + jnp.where(in_page < rest, widen(ending), 0.0)
    out[:, 0:tokens] = jnp.where(count > 0.5, jnp.log2(jnp.maximum(count, 1.0)), NEG)
    out[:, tokens:] = jnp.where((r // steps == c // steps) & (c <= r), 0.0, NEG)


def make_bias(table, length, steps):
    rows = table.shape[1]
    return pl.pallas_call(
        bias_kernel,
        out_shape=jax.ShapeDtypeStruct((rows * steps, POOL_SLOTS * PAGE + rows * steps), jnp.float32),
        in_specs=[VMEM] * 2,
        out_specs=VMEM,
        compiler_params=pltpu.CompilerParams(vmem_limit_bytes=VMEM_BYTES),
        name="bias",
    )(table, length)


def decode_kernel(pages, perm, bias, q_ref, fresh, pool, weight, theirs, mine, pool_out, *scratch):
    w_s, o_s, qs, attn, sems = scratch
    tp = lax.axis_index("tp")
    core, far = tp & 1, tp >> 1
    rows = q_ref.shape[0]
    wide = w_s.shape[1] // TILES
    loads = []
    for t in range(TILES):
        cols = pl.ds(t * wide, wide)
        loads.append(pltpu.make_async_copy(weight.at[:, cols], w_s.at[:, cols], sems.at[t]))
        loads[-1].start()

    slots = perm.shape[1]
    flags = pages[:, 2 * CAP * PAGE :, :].reshape(N_CTX * PAGE, HEAD)
    first = hot(iota((N_CTX, N_CTX * PAGE), 1) == iota((N_CTX, N_CTX * PAGE), 0) * PAGE)
    sent = dot(first, flags)[:, 0:slots]
    lane = iota((N_CTX, slots), 1)
    there = (lane // CAP == iota((N_CTX, slots), 0)) & (sent > (lane % CAP).astype(jnp.float32) + 0.5)
    there = jnp.sum(jnp.where(there, 1.0, 0.0), axis=0, keepdims=True)
    earlier = hot(iota((slots, slots), 0) < iota((slots, slots), 1))
    rank = dot(jnp.broadcast_to(there, (8, slots)).astype(jnp.bfloat16), earlier)[0:1, :]
    by_rank = hot((iota((slots, slots), 0).astype(jnp.float32) == rank) & (there > 0.5))
    by_slot = hot(iota((slots, slots), 0) == perm[...])
    moves = dot(by_slot, by_rank).astype(jnp.bfloat16)
    tokens = slots * PAGE
    spread = hot(iota((slots, tokens), 1) // PAGE == iota((slots, tokens), 0))
    spread_t = hot(iota((tokens, slots), 0) // PAGE == iota((tokens, slots), 1))
    tall = dot(spread_t, moves)
    replaced = jnp.sum(tall, axis=1, keepdims=True) > 0.5
    full = dot(tall.astype(jnp.bfloat16), spread)
    pick = hot((full > 0.5) & (iota((tokens, tokens), 0) % PAGE == iota((tokens, tokens), 1) % PAGE))
    got_k = pages[:, 0 : CAP * PAGE, :].reshape(tokens, HEAD)
    got_v = pages[:, CAP * PAGE : 2 * CAP * PAGE, :].reshape(tokens, HEAD)
    new = dot(pick, jnp.concatenate([got_k, got_v], axis=1))
    pool_out[0] = jnp.where(replaced, new[:, 0:HEAD], pool[0].astype(jnp.float32)).astype(jnp.bfloat16)
    pool_out[1] = jnp.where(replaced, new[:, HEAD:], pool[1].astype(jnp.float32)).astype(jnp.bfloat16)

    split_queries(q_ref, qs)
    k = jnp.concatenate([pool_out[0], fresh[0]], axis=0)
    v = jnp.concatenate([pool_out[1], fresh[1]], axis=0)
    k2 = jnp.concatenate([k, k], axis=1)
    v2 = jnp.concatenate([v, jnp.ones_like(v)], axis=1)
    scores, weights = {}, {}
    for t in range(HEADS + 2):
        if t < HEADS:
            scores[t] = lax.dot_general(
                qs[t * TOK : (t + 1) * TOK, :], k2, (((1,), (1,)), ((), ())), preferred_element_type=jnp.float32
            )
        if 0 <= t - 1 < HEADS:
            s = scores.pop(t - 1) + bias[...]
            weights[t - 1] = jnp.exp2(s - jnp.max(s, axis=1, keepdims=True)).astype(jnp.bfloat16)
        if 0 <= t - 2 < HEADS:
            o = dot(weights.pop(t - 2), v2)
            attn[:, (t - 2) * HEAD : (t - 1) * HEAD] = (o[:, 0:HEAD] / o[:, HEAD:]).astype(jnp.bfloat16)

    share = rows // 4
    part = lambda hi, lo: attn[pl.ds(pl.multiple_of((hi * 2 + lo) * share, share), share), :]
    rows_in = jnp.concatenate([part(1 - far, 1 - core), part(far, 1 - core), part(1 - far, core), part(far, core)])
    stores = []
    for t in range(TILES):
        loads[t].wait()
        cols = pl.ds(t * wide, wide)
        o_s[:, t * wide : (t + 1) * wide] = dot(rows_in, w_s[:, t * wide : (t + 1) * wide]).astype(jnp.bfloat16)
        for i, ref in enumerate((theirs, mine)):
            stores.append(
                pltpu.make_async_copy(
                    o_s.at[pl.ds(i * 2 * share, 2 * share), cols], ref.at[:, cols], sems.at[TILES + 2 * t + i]
                )
            )
            stores[-1].start()
    for store in stores:
        store.wait()


def decode(pages, perm, bias, q, fresh, pool, weight):
    rows = q.shape[0]
    keys = pool.shape[1] + rows
    depth, width = weight.shape
    return pl.pallas_call(
        decode_kernel,
        out_shape=(
            jax.ShapeDtypeStruct((rows // 2, width), jnp.bfloat16),
            jax.ShapeDtypeStruct((rows // 2, width), jnp.bfloat16),
            jax.ShapeDtypeStruct(pool.shape, jnp.bfloat16),
        ),
        in_specs=[VMEM] * 6 + [ANY],
        out_specs=(ANY, ANY, VMEM),
        scratch_shapes=[
            pltpu.VMEM((depth, width), jnp.bfloat16),
            pltpu.VMEM((rows, width), jnp.bfloat16),
            pltpu.VMEM((HEADS * rows, 2 * HEAD), jnp.bfloat16),
            pltpu.VMEM(q.shape, jnp.bfloat16),
            pltpu.SemaphoreType.DMA((3 * TILES,)),
        ],
        compiler_params=pltpu.CompilerParams(vmem_limit_bytes=VMEM_BYTES),
        cost_estimate=pl.CostEstimate(
            flops=100 * rows * depth * width,
            bytes_accessed=300 * 2**20,
            transcendentals=HEADS * rows * keys,
        ),
        name="decode",
    )(pages, perm, bias, q, fresh, pool, weight)


def body(
    q_pre,
    prefill_key_value,
    kv_past,
    offset,
    page_dest,
    slot_perm,
    pool,
    tables,
    lengths,
    decode_query,
    decode_key_value,
    out_weight,
):

    outgoing, pack = prep(prefill_key_value, kv_past, page_dest)
    pack_x = send(pack, "x", 1)
    pages = lax.all_to_all(outgoing, "ctx", split_axis=0, concat_axis=0, tiled=True)
    q_below, q_above, q_far = send(q_pre, "z", 1), send(q_pre, "z", -1), send(q_pre, "z", 2)
    near = jnp.stack([pack, pack_x])
    arrays = (near, send(near, "y", 1), send(near, "y", -1), send(near, "y", 2))

    rows_dev, steps = decode_query.shape[0], decode_query.shape[1]
    rows = rows_dev * steps
    theirs, mine, new_pool = decode(
        pages,
        slot_perm,
        make_bias(tables.T, lengths, steps),
        decode_query.reshape(rows, -1),
        decode_key_value.reshape(2, rows, HEAD),
        pool,
        out_weight,
    )
    f32 = jnp.float32
    share = rows // 4

    o_below = flash(offset, q_below, arrays, 3, deps=(theirs, q_above, q_far))
    o_below, theirs = lax.optimization_barrier((o_below, theirs))
    p_below = send(o_below, "z", -1)
    got = lax.ppermute(theirs, "tp", [(0, 1), (1, 0), (2, 3), (3, 2)])
    o_above = flash(offset, q_above, arrays, 1, deps=(o_below,))
    p_above = send(o_above, "z", 1)
    away = (mine[:share].astype(f32) + got[:share].astype(f32)).astype(jnp.bfloat16)
    back = lax.ppermute(away, "tp", [(0, 2), (1, 3), (2, 0), (3, 1)])
    o_far = flash(offset, q_far, arrays, 2, deps=(o_above, away))
    p_far = send(o_far, "z", 2)
    o_own = flash(offset, q_pre, arrays, 0, deps=(o_far,))
    pre_out = combine([o_own, p_below, p_above, p_far])

    dec_out = (mine[share:].astype(f32) + got[share:].astype(f32) + back.astype(f32)).astype(jnp.bfloat16)
    dec_out = dec_out.reshape(share // steps, steps, -1)
    return (pre_out, new_pool, dec_out)


def solution(mesh):
    return jax.shard_map(
        body,
        mesh=mesh,
        in_specs=(
            P("ctx", "tp"),
            P(None, "ctx", "tp"),
            P(None, "ctx", "tp"),
            P(),
            P("ctx", None),
            P("ctx", None),
            P(None, "ctx", "tp"),
            P("ctx", None),
            P("ctx", None),
            P("ctx", None, "tp"),
            P(None, "ctx", None, "tp"),
            P("tp", None),
        ),
        out_specs=(P("ctx", "tp"), P(None, "ctx", "tp"), P(("ctx", "tp"), None, None)),
        check_vma=False,
    )
```

```python
import functools

import jax
import jax.numpy as jnp
from jax import lax
from jax.experimental import pallas as pl
from jax.experimental.pallas import tpu as pltpu
from jax.sharding import PartitionSpec as P

HEAD = 128
PAGE = 16
CAP = 2
N_CTX = 32
HEADS = 8
POOL_SLOTS = 64
TOK = 256
CHUNKS = 8
SCALE = (HEAD**-0.5) * 1.4426950408889634
NEG = -1e30
BIG = 2048
SMALL = 1024
VMEM_BYTES = 56 * 2**20

SMEM = pl.BlockSpec(memory_space=pltpu.SMEM)
VMEM = pl.BlockSpec(memory_space=pltpu.VMEM)
ANY = pl.BlockSpec(memory_space=pl.ANY)


def shift_perm(axis, step):
    pairs = []
    for i in range(N_CTX):
        x, y, z = i // 16, (i // 4) % 4, i % 4
        if axis == "x":
            x = (x + step) % 2
        elif axis == "y":
            y = (y + step) % 4
        else:
            z = (z + step) % 4
        pairs.append((i, x * 16 + y * 4 + z))
    return pairs


def send(v, axis, step):
    return lax.ppermute(v, "ctx", shift_perm(axis, step))


def iota(shape, dim):
    return lax.broadcasted_iota(jnp.int32, shape, dim)


def hot(mask):
    return jnp.where(mask, 1.0, 0.0).astype(jnp.bfloat16)


def dot(a, b):
    return jnp.dot(a, b, preferred_element_type=jnp.float32)


def prep_kernel(kv, past, dest_row, out, pack):
    pack[0] = kv[...]
    pack[1] = past[...]
    pages = dest_row.shape[1]
    hits = jnp.where(iota((N_CTX, pages), 0) == dest_row[...], 1.0, 0.0)
    before = hot(iota((pages, pages), 0) < iota((pages, pages), 1))
    rank = jnp.sum(hits * dot(hits.astype(jnp.bfloat16), before), axis=0, keepdims=True)
    key = dest_row[...].astype(jnp.float32) * CAP + rank
    key = jnp.broadcast_to(key, (8, pages)).astype(jnp.bfloat16)
    tokens = pages * PAGE
    spread = hot((iota((pages, tokens), 1) >> 4) == iota((pages, tokens), 0))
    target = dot(key, spread)[0:1, :] * PAGE + ((iota((1, tokens), 1) & 15)).astype(jnp.float32)
    rows = N_CTX * CAP * PAGE
    pick = hot(iota((rows, tokens), 0).astype(jnp.float32) == target)
    both = dot(pick, jnp.concatenate([kv[0], kv[1]], axis=1)).astype(jnp.bfloat16)
    out[:, 0 : CAP * PAGE, :] = both[:, 0:HEAD].reshape(N_CTX, CAP * PAGE, HEAD)
    out[:, CAP * PAGE : 2 * CAP * PAGE, :] = both[:, HEAD:].reshape(N_CTX, CAP * PAGE, HEAD)
    count = jnp.broadcast_to(jnp.sum(hits, axis=1, keepdims=True), (N_CTX, HEAD)).astype(jnp.bfloat16)
    repeat = hot((iota((N_CTX * PAGE, N_CTX), 0) >> 4) == iota((N_CTX * PAGE, N_CTX), 1))
    out[:, 2 * CAP * PAGE :, :] = dot(repeat, count).astype(jnp.bfloat16).reshape(N_CTX, PAGE, HEAD)


def prep(kv, past, page_dest):
    return pl.pallas_call(
        prep_kernel,
        out_shape=(
            jax.ShapeDtypeStruct((N_CTX, (2 * CAP + 1) * PAGE, HEAD), jnp.bfloat16),
            jax.ShapeDtypeStruct((2,) + kv.shape, jnp.bfloat16),
        ),
        in_specs=[VMEM] * 3,
        out_specs=(VMEM, VMEM),
        compiler_params=pltpu.CompilerParams(vmem_limit_bytes=VMEM_BYTES),
        name="prep",
    )(kv, past, page_dest.reshape(1, -1))


def split_queries(q_ref, qs):
    for h in range(HEADS):
        scaled = q_ref[:, h * HEAD : (h + 1) * HEAD].astype(jnp.float32) * SCALE
        high = scaled.astype(jnp.bfloat16)
        qs[h * TOK : (h + 1) * TOK, 0:HEAD] = high
        qs[h * TOK : (h + 1) * TOK, HEAD:] = (scaled - high.astype(jnp.float32)).astype(jnp.bfloat16)


def fold(qs, m_s, acc_s, k, v, ones, mask, fresh):
    k2 = jnp.concatenate([k, k], axis=1)
    v2 = jnp.concatenate([v, ones], axis=1)

    def score(h):
        s = lax.dot_general(
            qs[h * TOK : (h + 1) * TOK, :], k2, (((1,), (1,)), ((), ())), preferred_element_type=jnp.float32
        )
        if mask is None:
            return s
        return jnp.concatenate([jnp.where(mask, s[:, :TOK], NEG), s[:, TOK:]], axis=1)

    def soft(h, s):
        rows = slice(h * TOK, (h + 1) * TOK)
        if fresh:
            new = jnp.broadcast_to(jnp.max(s, axis=1, keepdims=True), (TOK, HEAD))
            m_s[rows, :] = new
            return jnp.exp2(s - new[:, 0:1]).astype(jnp.bfloat16), None
        old = m_s[rows, :]
        new = jnp.maximum(old, jnp.max(s, axis=1, keepdims=True))
        m_s[rows, :] = new
        return jnp.exp2(s - new[:, 0:1]).astype(jnp.bfloat16), jnp.exp2(old - new)

    def add(h, p, a):
        rows = slice(h * TOK, (h + 1) * TOK)
        if fresh:
            acc_s[rows, :] = dot(p, v2)
            return
        acc_s[rows, :] = acc_s[rows, :] * jnp.concatenate([a, a], axis=1) + dot(p, v2)

    scores, weights = {}, {}
    for t in range(HEADS + 2):
        if t < HEADS:
            scores[t] = score(t)
        if 0 <= t - 1 < HEADS:
            weights[t - 1] = soft(t - 1, scores.pop(t - 1))
        if 0 <= t - 2 < HEADS:
            add(t - 2, *weights.pop(t - 2))


def flash_kernel(dz, n_dep, offset_ref, q_ref, near, plus, minus, far, *refs):
    out, q_s, k_s, v_s, ones_s, qs, m_s, acc_s, sems = refs[n_dep:]
    me, offset = lax.axis_index("ctx"), offset_ref[0]
    x, y, z = me >> 4, (me >> 2) & 3, me & 3
    group = me >> 2
    zq = (z + dz) & 3
    get_q = pltpu.make_async_copy(q_ref, q_s, sems.at[4 * CHUNKS])
    get_q.start()
    seen = group + (1 if dz == 0 else (z < zq).astype(jnp.int32))

    def length(c):
        cached = jnp.clip(offset - (c * 4 + z) * TOK, 0, TOK)
        return jnp.where(c < CHUNKS, cached, jnp.where(c - CHUNKS < seen, TOK, 0))

    copies = []
    for s in (1, 0):
        for array, dy in ((near, 0), (plus, 3), (minus, 1), (far, 2)):
            for dx in range(2):
                j = (x ^ dx) * 4 + ((y + dy) & 3)
                if s == 1:
                    slot = j
                    live = length(j) > 0
                else:
                    place = jnp.where(j == group, 0, j + 1) if dz == 0 else j
                    slot = CHUNKS + place
                    live = place < seen if dz else j <= group
                row = pl.multiple_of(slot * TOK, TOK)
                n = len(copies)
                kc = pltpu.make_async_copy(array.at[dx, s, 0], k_s.at[pl.ds(row, TOK)], sems.at[2 * n])
                vc = pltpu.make_async_copy(array.at[dx, s, 1], v_s.at[pl.ds(row, TOK)], sems.at[2 * n + 1])
                copies.append((live, kc, vc))

                @pl.when(live)
                def _():
                    kc.start()
                    vc.start()

    ones_s[...] = jnp.ones_like(ones_s)
    get_q.wait()
    split_queries(q_s, qs)

    def fill(c, _):
        valid = length(c)

        @pl.when(valid < TOK)
        def _():
            inside = iota((TOK, HEAD), 0) < valid
            rows = pl.ds(pl.multiple_of(c * TOK, TOK), TOK)
            start = pl.multiple_of((c // CHUNKS) * BIG, BIG)
            first = k_s[pl.ds(start, 16), :][0:1, :].astype(jnp.float32)
            k_s[rows, :] = jnp.where(inside, k_s[rows, :].astype(jnp.float32), first).astype(jnp.bfloat16)
            v_s[rows, :] = jnp.where(inside, v_s[rows, :].astype(jnp.float32), 0.0).astype(jnp.bfloat16)
            ones_s[rows, :] = jnp.where(inside, 1.0, 0.0).astype(jnp.bfloat16)

        return 0

    cached = jnp.int32(0)
    for c in range(CHUNKS):
        cached = cached + length(c)
    diagonal = iota((TOK, TOK), 1) <= iota((TOK, TOK), 0) if dz == 0 else None
    for region, n, mask in ((0, cached, None), (1, seen * TOK, diagonal)):
        for live, kc, vc in copies[region * CHUNKS : (region + 1) * CHUNKS]:

            @pl.when(live)
            def _():
                kc.wait()
                vc.wait()

        lax.fori_loop(region * CHUNKS, (region + 1) * CHUNKS, fill, 0)
        for size in (SMALL, BIG):

            @pl.when((n > size - SMALL) & ((n <= size) | (size == BIG)))
            def _():
                rows = slice(region * BIG, region * BIG + size)
                fold(qs, m_s, acc_s, k_s[rows, :], v_s[rows, :], ones_s[rows, :], mask, region == 0)

    lane = iota((TOK, HEAD), 1)
    level = jnp.zeros((TOK, HEAD), jnp.float32)
    for h in range(HEADS):
        rows = slice(h * TOK, (h + 1) * TOK)
        total = acc_s[rows, HEAD:]
        out[:, h * HEAD : (h + 1) * HEAD] = (acc_s[rows, 0:HEAD] / total).astype(jnp.bfloat16)
        value = m_s[rows, :] + jnp.log2(total)
        high = value.astype(jnp.bfloat16).astype(jnp.float32)
        middle = (value - high).astype(jnp.bfloat16).astype(jnp.float32)
        low = value - high - middle
        level = jnp.where(lane == h, high, level)
        level = jnp.where(lane == HEADS + h, middle, level)
        level = jnp.where(lane == 2 * HEADS + h, low, level)
    out[:, HEADS * HEAD :] = level.astype(jnp.bfloat16)


def flash(offset, q, arrays, dz, deps=()):
    work = 2 * CHUNKS * TOK * TOK * HEADS
    rows = 2 * CHUNKS * TOK
    return pl.pallas_call(
        functools.partial(flash_kernel, dz, len(deps)),
        out_shape=jax.ShapeDtypeStruct((TOK, HEADS * HEAD + HEAD), jnp.bfloat16),
        in_specs=[SMEM] + [ANY] * (5 + len(deps)),
        out_specs=VMEM,
        scratch_shapes=[
            pltpu.VMEM((TOK, HEADS * HEAD), jnp.bfloat16),
            pltpu.VMEM((rows, HEAD), jnp.bfloat16),
            pltpu.VMEM((rows, HEAD), jnp.bfloat16),
            pltpu.VMEM((rows, HEAD), jnp.bfloat16),
            pltpu.VMEM((HEADS * TOK, 2 * HEAD), jnp.bfloat16),
            pltpu.VMEM((HEADS * TOK, HEAD), jnp.float32),
            pltpu.VMEM((HEADS * TOK, 2 * HEAD), jnp.float32),
            pltpu.SemaphoreType.DMA((4 * CHUNKS + 1,)),
        ],
        compiler_params=pltpu.CompilerParams(vmem_limit_bytes=VMEM_BYTES),
        cost_estimate=pl.CostEstimate(flops=work * HEAD * 8, bytes_accessed=3 * 2**20, transcendentals=work),
        name=f"flash{dz}",
    )(offset, q, *arrays, *deps)


def combine_kernel(*refs):
    parts, out = refs[:-1], refs[-1]
    width = HEADS * HEAD
    levels = []
    for part in parts:
        three = part[:, width:].astype(jnp.float32)
        levels.append(three[:, 0:HEADS] + three[:, HEADS : 2 * HEADS] + three[:, 2 * HEADS : 3 * HEADS])
    top = functools.reduce(jnp.maximum, levels)
    shares = [jnp.exp2(v - top) for v in levels]
    total = functools.reduce(jnp.add, shares)
    shares = [s / total for s in shares]
    for h in range(HEADS):
        cols = slice(h * HEAD, (h + 1) * HEAD)
        acc = jnp.zeros((TOK, HEAD), jnp.float32)
        for part, share in zip(parts, shares):
            acc = acc + part[:, cols].astype(jnp.float32) * share[:, h : h + 1]
        out[:, cols] = acc.astype(jnp.bfloat16)


def combine(parts):
    return pl.pallas_call(
        combine_kernel,
        out_shape=jax.ShapeDtypeStruct((TOK, HEADS * HEAD), jnp.bfloat16),
        in_specs=[VMEM] * len(parts),
        out_specs=VMEM,
        compiler_params=pltpu.CompilerParams(vmem_limit_bytes=VMEM_BYTES),
        name="combine",
    )(*parts)


TILES = 4


def bias_kernel(table, length, out):
    pages, rows = table.shape
    slots, steps = POOL_SLOTS, out.shape[0] // rows
    tokens, all_rows = slots * PAGE, rows * steps
    live = length[...]
    whole = live >> 4
    slot_id = iota((slots, rows), 0)
    times = jnp.zeros((slots, rows), jnp.float32)
    ending = jnp.zeros((slots, rows), jnp.float32)
    for a in range(pages):
        hit = table[a : a + 1, :] == slot_id
        times = times + jnp.where(hit & (whole > a), 1.0, 0.0)
        ending = ending + jnp.where(hit & (whole == a), 1.0, 0.0)
    repeat = hot(iota((rows, all_rows), 0) == (iota((rows, all_rows), 1) >> 2))
    spread = hot((iota((slots, tokens), 1) >> 4) == iota((slots, tokens), 0))
    rest = jnp.broadcast_to((live & 15).astype(jnp.float32), (8, rows)).astype(jnp.bfloat16)
    rest = dot(rest, repeat)[0:1, :]
    r, c = iota((all_rows, all_rows), 0), iota((all_rows, all_rows), 1)
    rest = jnp.sum(jnp.where(r == c, rest, 0.0), axis=1, keepdims=True)

    def widen(v):
        v = dot(v.astype(jnp.bfloat16), repeat).astype(jnp.bfloat16)
        return lax.dot_general(v, spread, (((0,), (0,)), ((), ())), preferred_element_type=jnp.float32)

    in_page = ((iota((all_rows, tokens), 1) & 15)).astype(jnp.float32)
    count = widen(times) + jnp.where(in_page < rest, widen(ending), 0.0)
    out[:, 0:tokens] = jnp.where(count > 0.5, jnp.log2(jnp.maximum(count, 1.0)), NEG)
    out[:, tokens:] = jnp.where(((r >> 2) == (c >> 2)) & (c <= r), 0.0, NEG)


def make_bias(table, length, steps):
    rows = table.shape[1]
    return pl.pallas_call(
        bias_kernel,
        out_shape=jax.ShapeDtypeStruct((rows * steps, POOL_SLOTS * PAGE + rows * steps), jnp.float32),
        in_specs=[VMEM] * 2,
        out_specs=VMEM,
        compiler_params=pltpu.CompilerParams(vmem_limit_bytes=VMEM_BYTES),
        name="bias",
    )(table, length)


def decode_kernel(pages, perm, bias, q_ref, fresh, pool, weight, theirs, mine, pool_out, *scratch):
    w_s, o_s, qs, attn, sems = scratch
    tp = lax.axis_index("tp")
    core, far = tp & 1, tp >> 1
    rows = q_ref.shape[0]
    wide = w_s.shape[1] // TILES
    loads = []
    for t in range(TILES):
        cols = pl.ds(t * wide, wide)
        loads.append(pltpu.make_async_copy(weight.at[:, cols], w_s.at[:, cols], sems.at[t]))
        loads[-1].start()

    slots = perm.shape[1]
    flags = pages[:, 2 * CAP * PAGE :, :].reshape(N_CTX * PAGE, HEAD)
    first = hot(iota((N_CTX, N_CTX * PAGE), 1) == iota((N_CTX, N_CTX * PAGE), 0) * PAGE)
    sent = dot(first, flags)[:, 0:slots]
    lane = iota((N_CTX, slots), 1)
    there = ((lane >> 1) == iota((N_CTX, slots), 0)) & (sent > (lane & 1).astype(jnp.float32) + 0.5)
    there = jnp.sum(jnp.where(there, 1.0, 0.0), axis=0, keepdims=True)
    earlier = hot(iota((slots, slots), 0) < iota((slots, slots), 1))
    rank = dot(jnp.broadcast_to(there, (8, slots)).astype(jnp.bfloat16), earlier)[0:1, :]
    by_rank = hot((iota((slots, slots), 0).astype(jnp.float32) == rank) & (there > 0.5))
    by_slot = hot(iota((slots, slots), 0) == perm[...])
    moves = dot(by_slot, by_rank).astype(jnp.bfloat16)
    tokens = slots * PAGE
    spread = hot((iota((slots, tokens), 1) >> 4) == iota((slots, tokens), 0))
    spread_t = hot((iota((tokens, slots), 0) >> 4) == iota((tokens, slots), 1))
    tall = dot(spread_t, moves)
    replaced = jnp.sum(tall, axis=1, keepdims=True) > 0.5
    full = dot(tall.astype(jnp.bfloat16), spread)
    pick = hot((full > 0.5) & (((iota((tokens, tokens), 0) ^ iota((tokens, tokens), 1)) & 15) == 0))
    got_k = pages[:, 0 : CAP * PAGE, :].reshape(tokens, HEAD)
    got_v = pages[:, CAP * PAGE : 2 * CAP * PAGE, :].reshape(tokens, HEAD)
    new = dot(pick, jnp.concatenate([got_k, got_v], axis=1))
    pool_out[0] = jnp.where(replaced, new[:, 0:HEAD], pool[0].astype(jnp.float32)).astype(jnp.bfloat16)
    pool_out[1] = jnp.where(replaced, new[:, HEAD:], pool[1].astype(jnp.float32)).astype(jnp.bfloat16)

    split_queries(q_ref, qs)
    k = jnp.concatenate([pool_out[0], fresh[0]], axis=0)
    v = jnp.concatenate([pool_out[1], fresh[1]], axis=0)
    k2 = jnp.concatenate([k, k], axis=1)
    v2 = jnp.concatenate([v, jnp.ones_like(v)], axis=1)
    scores, weights = {}, {}
    for t in range(HEADS + 2):
        if t < HEADS:
            scores[t] = lax.dot_general(
                qs[t * TOK : (t + 1) * TOK, :], k2, (((1,), (1,)), ((), ())), preferred_element_type=jnp.float32
            )
        if 0 <= t - 1 < HEADS:
            s = scores.pop(t - 1) + bias[...]
            weights[t - 1] = jnp.exp2(s - jnp.max(s, axis=1, keepdims=True)).astype(jnp.bfloat16)
        if 0 <= t - 2 < HEADS:
            o = dot(weights.pop(t - 2), v2)
            attn[:, (t - 2) * HEAD : (t - 1) * HEAD] = (o[:, 0:HEAD] / o[:, HEAD:]).astype(jnp.bfloat16)

    share = rows // 4
    part = lambda hi, lo: attn[pl.ds(pl.multiple_of((hi * 2 + lo) * share, share), share), :]
    rows_in = jnp.concatenate([part(1 - far, 1 - core), part(far, 1 - core), part(1 - far, core), part(far, core)])
    stores = []
    for t in range(TILES):
        loads[t].wait()
        cols = pl.ds(t * wide, wide)
        o_s[:, t * wide : (t + 1) * wide] = dot(rows_in, w_s[:, t * wide : (t + 1) * wide]).astype(jnp.bfloat16)
        for i, ref in enumerate((theirs, mine)):
            stores.append(
                pltpu.make_async_copy(
                    o_s.at[pl.ds(i * 2 * share, 2 * share), cols], ref.at[:, cols], sems.at[TILES + 2 * t + i]
                )
            )
            stores[-1].start()
    for store in stores:
        store.wait()


def decode(pages, perm, bias, q, fresh, pool, weight):
    rows = q.shape[0]
    keys = pool.shape[1] + rows
    depth, width = weight.shape
    return pl.pallas_call(
        decode_kernel,
        out_shape=(
            jax.ShapeDtypeStruct((rows // 2, width), jnp.bfloat16),
            jax.ShapeDtypeStruct((rows // 2, width), jnp.bfloat16),
            jax.ShapeDtypeStruct(pool.shape, jnp.bfloat16),
        ),
        in_specs=[VMEM] * 6 + [ANY],
        out_specs=(ANY, ANY, VMEM),
        scratch_shapes=[
            pltpu.VMEM((depth, width), jnp.bfloat16),
            pltpu.VMEM((rows, width), jnp.bfloat16),
            pltpu.VMEM((HEADS * rows, 2 * HEAD), jnp.bfloat16),
            pltpu.VMEM(q.shape, jnp.bfloat16),
            pltpu.SemaphoreType.DMA((3 * TILES,)),
        ],
        compiler_params=pltpu.CompilerParams(vmem_limit_bytes=VMEM_BYTES),
        cost_estimate=pl.CostEstimate(
            flops=100 * rows * depth * width,
            bytes_accessed=300 * 2**20,
            transcendentals=HEADS * rows * keys,
        ),
        name="decode",
    )(pages, perm, bias, q, fresh, pool, weight)


def body(
    q_pre,
    prefill_key_value,
    kv_past,
    offset,
    page_dest,
    slot_perm,
    pool,
    tables,
    lengths,
    decode_query,
    decode_key_value,
    out_weight,
):

    rows_dev, steps = decode_query.shape[0], decode_query.shape[1]
    rows = rows_dev * steps
    bias = make_bias(tables.T, lengths, steps)
    dec_q = decode_query.reshape(rows, -1)
    fresh = decode_key_value.reshape(2, rows, HEAD)

    outgoing, pack = prep(prefill_key_value, kv_past, page_dest)
    pages = lax.all_to_all(outgoing, "ctx", split_axis=0, concat_axis=0, tiled=True)
    near = jnp.stack([pack, send(pack, "x", 1)])
    arrays = (near, send(near, "y", 1), send(near, "y", -1), send(near, "y", 2))
    q_below, q_above, q_far = send(q_pre, "z", 1), send(q_pre, "z", -1), send(q_pre, "z", 2)

    theirs, mine, new_pool = decode(pages, slot_perm, bias, dec_q, fresh, pool, out_weight)
    f32 = jnp.float32
    share = rows // 4

    o_above = flash(offset, q_above, arrays, 1, deps=(theirs, q_far))
    o_above, theirs = lax.optimization_barrier((o_above, theirs))
    p_above = send(o_above, "z", 1)
    got = lax.ppermute(theirs, "tp", [(0, 1), (1, 0), (2, 3), (3, 2)])
    o_far = flash(offset, q_far, arrays, 2, deps=(o_above,))
    p_far = send(o_far, "z", 2)
    away = (mine[:share].astype(f32) + got[:share].astype(f32)).astype(jnp.bfloat16)
    back = lax.ppermute(away, "tp", [(0, 2), (1, 3), (2, 0), (3, 1)])
    o_below = flash(offset, q_below, arrays, 3, deps=(o_far, away))
    p_below = send(o_below, "z", -1)
    o_own = flash(offset, q_pre, arrays, 0, deps=(o_below,))
    pre_out = combine([o_own, p_above, p_far, p_below])

    dec_out = (mine[share:].astype(f32) + got[share:].astype(f32) + back.astype(f32)).astype(jnp.bfloat16)
    dec_out = dec_out.reshape(share // steps, steps, -1)
    return (pre_out, new_pool, dec_out)


def solution(mesh):
    return jax.shard_map(
        body,
        mesh=mesh,
        in_specs=(
            P("ctx", "tp"),
            P(None, "ctx", "tp"),
            P(None, "ctx", "tp"),
            P(),
            P("ctx", None),
            P("ctx", None),
            P(None, "ctx", "tp"),
            P("ctx", None),
            P("ctx", None),
            P("ctx", None, "tp"),
            P(None, "ctx", None, "tp"),
            P("tp", None),
        ),
        out_specs=(P("ctx", "tp"), P(None, "ctx", "tp"), P(("ctx", "tp"), None, None)),
        check_vma=False,
    )
```

```python
import functools

import jax
import jax.numpy as jnp
from jax import lax
from jax.experimental import pallas as pl
from jax.experimental.pallas import tpu as pltpu
from jax.sharding import PartitionSpec as P

HEAD = 128
PAGE = 16
CAP = 2
N_CTX = 32
HEADS = 8
POOL_SLOTS = 64
TOK = 256
CHUNKS = 8
SCALE = (HEAD**-0.5) * 1.4426950408889634
NEG = -1e30
SIZES = (7, 8)
VMEM_BYTES = 56 * 2**20

SMEM = pl.BlockSpec(memory_space=pltpu.SMEM)
VMEM = pl.BlockSpec(memory_space=pltpu.VMEM)
ANY = pl.BlockSpec(memory_space=pl.ANY)


def shift_perm(axis, step):
    pairs = []
    for i in range(N_CTX):
        x, y, z = i // 16, (i // 4) % 4, i % 4
        if axis == "x":
            x = (x + step) % 2
        elif axis == "y":
            y = (y + step) % 4
        else:
            z = (z + step) % 4
        pairs.append((i, x * 16 + y * 4 + z))
    return pairs


def send(v, axis, step):
    return lax.ppermute(v, "ctx", shift_perm(axis, step))


def iota(shape, dim):
    return lax.broadcasted_iota(jnp.int32, shape, dim)


def hot(mask):
    return jnp.where(mask, 1.0, 0.0).astype(jnp.bfloat16)


def dot(a, b):
    return jnp.dot(a, b, preferred_element_type=jnp.float32)


def prep_kernel(kv, past, dest_row, out, pack):
    pack[0] = kv[...]
    pack[1] = past[...]
    pages = dest_row.shape[1]
    hits = jnp.where(iota((N_CTX, pages), 0) == dest_row[...], 1.0, 0.0)
    before = hot(iota((pages, pages), 0) < iota((pages, pages), 1))
    rank = jnp.sum(hits * dot(hits.astype(jnp.bfloat16), before), axis=0, keepdims=True)
    key = dest_row[...].astype(jnp.float32) * CAP + rank
    key = jnp.broadcast_to(key, (8, pages)).astype(jnp.bfloat16)
    tokens = pages * PAGE
    spread = hot((iota((pages, tokens), 1) >> 4) == iota((pages, tokens), 0))
    target = dot(key, spread)[0:1, :] * PAGE + ((iota((1, tokens), 1) & 15)).astype(jnp.float32)
    rows = N_CTX * CAP * PAGE
    pick = hot(iota((rows, tokens), 0).astype(jnp.float32) == target)
    both = dot(pick, jnp.concatenate([kv[0], kv[1]], axis=1)).astype(jnp.bfloat16)
    out[:, 0 : CAP * PAGE, :] = both[:, 0:HEAD].reshape(N_CTX, CAP * PAGE, HEAD)
    out[:, CAP * PAGE : 2 * CAP * PAGE, :] = both[:, HEAD:].reshape(N_CTX, CAP * PAGE, HEAD)
    count = jnp.broadcast_to(jnp.sum(hits, axis=1, keepdims=True), (N_CTX, HEAD)).astype(jnp.bfloat16)
    repeat = hot((iota((N_CTX * PAGE, N_CTX), 0) >> 4) == iota((N_CTX * PAGE, N_CTX), 1))
    out[:, 2 * CAP * PAGE :, :] = dot(repeat, count).astype(jnp.bfloat16).reshape(N_CTX, PAGE, HEAD)


def prep(kv, past, page_dest):
    return pl.pallas_call(
        prep_kernel,
        out_shape=(
            jax.ShapeDtypeStruct((N_CTX, (2 * CAP + 1) * PAGE, HEAD), jnp.bfloat16),
            jax.ShapeDtypeStruct((2,) + kv.shape, jnp.bfloat16),
        ),
        in_specs=[VMEM] * 3,
        out_specs=(VMEM, VMEM),
        compiler_params=pltpu.CompilerParams(vmem_limit_bytes=VMEM_BYTES),
        name="prep",
    )(kv, past, page_dest.reshape(1, -1))


def split_queries(q_ref, qs):
    for h in range(HEADS):
        scaled = q_ref[:, h * HEAD : (h + 1) * HEAD].astype(jnp.float32) * SCALE
        high = scaled.astype(jnp.bfloat16)
        qs[h * TOK : (h + 1) * TOK, 0:HEAD] = high
        qs[h * TOK : (h + 1) * TOK, HEAD:] = (scaled - high.astype(jnp.float32)).astype(jnp.bfloat16)


def fold(qs, m_s, acc_s, k, v, ones, mask=None):
    k2 = jnp.concatenate([k, k], axis=1)
    v2 = jnp.concatenate([v, ones], axis=1)

    def score(h):
        s = lax.dot_general(
            qs[h * TOK : (h + 1) * TOK, :], k2, (((1,), (1,)), ((), ())), preferred_element_type=jnp.float32
        )
        if mask is None:
            return s
        return jnp.concatenate([jnp.where(mask, s[:, :TOK], NEG), s[:, TOK:]], axis=1)

    def soft(h, s):
        rows = slice(h * TOK, (h + 1) * TOK)
        old = m_s[rows, :]
        new = jnp.maximum(old, jnp.max(s, axis=1, keepdims=True))
        m_s[rows, :] = new
        return jnp.exp2(s - new[:, 0:1]).astype(jnp.bfloat16), jnp.exp2(old - new)

    def add(h, p, a):
        rows = slice(h * TOK, (h + 1) * TOK)
        acc_s[rows, :] = acc_s[rows, :] * jnp.concatenate([a, a], axis=1) + dot(p, v2)

    scores, weights = {}, {}
    for t in range(HEADS + 2):
        if t < HEADS:
            scores[t] = score(t)
        if 0 <= t - 1 < HEADS:
            weights[t - 1] = soft(t - 1, scores.pop(t - 1))
        if 0 <= t - 2 < HEADS:
            add(t - 2, *weights.pop(t - 2))


def flash_kernel(dz, n_dep, offset_ref, q_ref, near, plus, minus, far, *refs):
    out, q_s, k_s, v_s, ones_s, qs, m_s, acc_s, sems = refs[n_dep:]
    me, offset = lax.axis_index("ctx"), offset_ref[0]
    x, y, z = me >> 4, (me >> 2) & 3, me & 3
    group = me >> 2
    zq = (z + dz) & 3
    get_q = pltpu.make_async_copy(q_ref, q_s, sems.at[4 * CHUNKS])
    get_q.start()
    seen = group + (1 if dz == 0 else (z < zq).astype(jnp.int32))
    count = seen * TOK
    copies = []
    for s in (0, 1):
        for array, dy in ((near, 0), (plus, 3), (minus, 1), (far, 2)):
            for dx in range(2):
                j = (x ^ dx) * 4 + ((y + dy) & 3)
                if s == 0:
                    slot = jnp.where(j == group, 0, j + 1) if dz == 0 else j
                    live = slot < seen if dz else j <= group
                else:
                    length = jnp.clip(offset - (j * 4 + z) * TOK, 0, TOK)
                    count = count + length
                    slot = seen + j
                    live = length > 0
                row = pl.multiple_of(slot * TOK, TOK)
                n = len(copies)
                kc = pltpu.make_async_copy(array.at[dx, s, 0], k_s.at[pl.ds(row, TOK)], sems.at[2 * n])
                vc = pltpu.make_async_copy(array.at[dx, s, 1], v_s.at[pl.ds(row, TOK)], sems.at[2 * n + 1])
                copies.append((live, kc, vc))

                @pl.when(live)
                def _():
                    kc.start()
                    vc.start()

    ones_s[...] = jnp.ones_like(ones_s)
    m_s[...] = jnp.full_like(m_s, NEG)
    acc_s[...] = jnp.zeros_like(acc_s)
    get_q.wait()
    split_queries(q_s, qs)
    for live, kc, vc in copies:

        @pl.when(live)
        def _():
            kc.wait()
            vc.wait()

    size = jnp.int32(SIZES[-1])
    for chunks in SIZES[-2::-1]:
        size = jnp.where(count <= 2 * TOK * chunks, chunks, size)

    def fill(c, _):
        inside = iota((TOK, HEAD), 0) < count - c * TOK
        rows = pl.ds(pl.multiple_of(c * TOK, TOK), TOK)
        first = k_s[0:16, :][0:1, :].astype(jnp.float32)
        k_s[rows, :] = jnp.where(inside, k_s[rows, :].astype(jnp.float32), first).astype(jnp.bfloat16)
        v_s[rows, :] = jnp.where(inside, v_s[rows, :].astype(jnp.float32), 0.0).astype(jnp.bfloat16)
        ones_s[rows, :] = jnp.where(inside, 1.0, 0.0).astype(jnp.bfloat16)
        return 0

    lax.fori_loop(count >> 8, 2 * size, fill, 0)
    diagonal = iota((TOK, TOK), 1) <= iota((TOK, TOK), 0)

    def step(i, _):
        for chunks in SIZES:

            @pl.when(size == chunks)
            def _():
                rows = pl.ds(pl.multiple_of(i * (chunks * TOK), TOK), chunks * TOK)
                mask = diagonal | (i > 0) if dz == 0 else None
                fold(qs, m_s, acc_s, k_s[rows, :], v_s[rows, :], ones_s[rows, :], mask)

        return 0

    lax.fori_loop(0, 2, step, 0)

    lane = iota((TOK, HEAD), 1)
    level = jnp.zeros((TOK, HEAD), jnp.float32)
    for h in range(HEADS):
        rows = slice(h * TOK, (h + 1) * TOK)
        total = acc_s[rows, HEAD:]
        out[:, h * HEAD : (h + 1) * HEAD] = (acc_s[rows, 0:HEAD] / total).astype(jnp.bfloat16)
        value = m_s[rows, :] + jnp.log2(total)
        high = value.astype(jnp.bfloat16).astype(jnp.float32)
        middle = (value - high).astype(jnp.bfloat16).astype(jnp.float32)
        low = value - high - middle
        level = jnp.where(lane == h, high, level)
        level = jnp.where(lane == HEADS + h, middle, level)
        level = jnp.where(lane == 2 * HEADS + h, low, level)
    out[:, HEADS * HEAD :] = level.astype(jnp.bfloat16)


def flash(offset, q, arrays, dz, deps=()):
    work = 2 * CHUNKS * TOK * TOK * HEADS
    rows = 2 * CHUNKS * TOK
    return pl.pallas_call(
        functools.partial(flash_kernel, dz, len(deps)),
        out_shape=jax.ShapeDtypeStruct((TOK, HEADS * HEAD + HEAD), jnp.bfloat16),
        in_specs=[SMEM] + [ANY] * (5 + len(deps)),
        out_specs=VMEM,
        scratch_shapes=[
            pltpu.VMEM((TOK, HEADS * HEAD), jnp.bfloat16),
            pltpu.VMEM((rows, HEAD), jnp.bfloat16),
            pltpu.VMEM((rows, HEAD), jnp.bfloat16),
            pltpu.VMEM((rows, HEAD), jnp.bfloat16),
            pltpu.VMEM((HEADS * TOK, 2 * HEAD), jnp.bfloat16),
            pltpu.VMEM((HEADS * TOK, HEAD), jnp.float32),
            pltpu.VMEM((HEADS * TOK, 2 * HEAD), jnp.float32),
            pltpu.SemaphoreType.DMA((4 * CHUNKS + 1,)),
        ],
        compiler_params=pltpu.CompilerParams(vmem_limit_bytes=VMEM_BYTES),
        cost_estimate=pl.CostEstimate(flops=work * HEAD * 8, bytes_accessed=3 * 2**20, transcendentals=work),
        name=f"flash{dz}",
    )(offset, q, *arrays, *deps)


def combine_kernel(*refs):
    parts, out = refs[:-1], refs[-1]
    width = HEADS * HEAD
    levels = []
    for part in parts:
        three = part[:, width:].astype(jnp.float32)
        levels.append(three[:, 0:HEADS] + three[:, HEADS : 2 * HEADS] + three[:, 2 * HEADS : 3 * HEADS])
    top = functools.reduce(jnp.maximum, levels)
    shares = [jnp.exp2(v - top) for v in levels]
    total = functools.reduce(jnp.add, shares)
    shares = [s / total for s in shares]
    for h in range(HEADS):
        cols = slice(h * HEAD, (h + 1) * HEAD)
        acc = jnp.zeros((TOK, HEAD), jnp.float32)
        for part, share in zip(parts, shares):
            acc = acc + part[:, cols].astype(jnp.float32) * share[:, h : h + 1]
        out[:, cols] = acc.astype(jnp.bfloat16)


def combine(parts):
    return pl.pallas_call(
        combine_kernel,
        out_shape=jax.ShapeDtypeStruct((TOK, HEADS * HEAD), jnp.bfloat16),
        in_specs=[VMEM] * len(parts),
        out_specs=VMEM,
        compiler_params=pltpu.CompilerParams(vmem_limit_bytes=VMEM_BYTES),
        name="combine",
    )(*parts)


TILES = 4


def bias_kernel(table, length, out):
    pages, rows = table.shape
    slots, steps = POOL_SLOTS, out.shape[0] // rows
    tokens, all_rows = slots * PAGE, rows * steps
    live = length[...]
    whole = live >> 4
    slot_id = iota((slots, rows), 0)
    times = jnp.zeros((slots, rows), jnp.float32)
    ending = jnp.zeros((slots, rows), jnp.float32)
    for a in range(pages):
        hit = table[a : a + 1, :] == slot_id
        times = times + jnp.where(hit & (whole > a), 1.0, 0.0)
        ending = ending + jnp.where(hit & (whole == a), 1.0, 0.0)
    repeat = hot(iota((rows, all_rows), 0) == (iota((rows, all_rows), 1) >> 2))
    spread = hot((iota((slots, tokens), 1) >> 4) == iota((slots, tokens), 0))
    rest = jnp.broadcast_to((live & 15).astype(jnp.float32), (8, rows)).astype(jnp.bfloat16)
    rest = dot(rest, repeat)[0:1, :]
    r, c = iota((all_rows, all_rows), 0), iota((all_rows, all_rows), 1)
    rest = jnp.sum(jnp.where(r == c, rest, 0.0), axis=1, keepdims=True)

    def widen(v):
        v = dot(v.astype(jnp.bfloat16), repeat).astype(jnp.bfloat16)
        return lax.dot_general(v, spread, (((0,), (0,)), ((), ())), preferred_element_type=jnp.float32)

    in_page = ((iota((all_rows, tokens), 1) & 15)).astype(jnp.float32)
    count = widen(times) + jnp.where(in_page < rest, widen(ending), 0.0)
    out[:, 0:tokens] = jnp.where(count > 0.5, jnp.log2(jnp.maximum(count, 1.0)), NEG)
    out[:, tokens:] = jnp.where(((r >> 2) == (c >> 2)) & (c <= r), 0.0, NEG)


def make_bias(table, length, steps):
    rows = table.shape[1]
    return pl.pallas_call(
        bias_kernel,
        out_shape=jax.ShapeDtypeStruct((rows * steps, POOL_SLOTS * PAGE + rows * steps), jnp.float32),
        in_specs=[VMEM] * 2,
        out_specs=VMEM,
        compiler_params=pltpu.CompilerParams(vmem_limit_bytes=VMEM_BYTES),
        name="bias",
    )(table, length)


def decode_kernel(pages, perm, bias, q_ref, fresh, pool, weight, theirs, mine, pool_out, *scratch):
    w_s, o_s, qs, attn, sems = scratch
    tp = lax.axis_index("tp")
    core, far = tp & 1, tp >> 1
    rows = q_ref.shape[0]
    wide = w_s.shape[1] // TILES
    loads = []
    for t in range(TILES):
        cols = pl.ds(t * wide, wide)
        loads.append(pltpu.make_async_copy(weight.at[:, cols], w_s.at[:, cols], sems.at[t]))
        loads[-1].start()

    slots = perm.shape[1]
    flags = pages[:, 2 * CAP * PAGE :, :].reshape(N_CTX * PAGE, HEAD)
    first = hot(iota((N_CTX, N_CTX * PAGE), 1) == iota((N_CTX, N_CTX * PAGE), 0) * PAGE)
    sent = dot(first, flags)[:, 0:slots]
    lane = iota((N_CTX, slots), 1)
    there = ((lane >> 1) == iota((N_CTX, slots), 0)) & (sent > (lane & 1).astype(jnp.float32) + 0.5)
    there = jnp.sum(jnp.where(there, 1.0, 0.0), axis=0, keepdims=True)
    earlier = hot(iota((slots, slots), 0) < iota((slots, slots), 1))
    rank = dot(jnp.broadcast_to(there, (8, slots)).astype(jnp.bfloat16), earlier)[0:1, :]
    by_rank = hot((iota((slots, slots), 0).astype(jnp.float32) == rank) & (there > 0.5))
    by_slot = hot(iota((slots, slots), 0) == perm[...])
    moves = dot(by_slot, by_rank).astype(jnp.bfloat16)
    tokens = slots * PAGE
    spread = hot((iota((slots, tokens), 1) >> 4) == iota((slots, tokens), 0))
    spread_t = hot((iota((tokens, slots), 0) >> 4) == iota((tokens, slots), 1))
    tall = dot(spread_t, moves)
    replaced = jnp.sum(tall, axis=1, keepdims=True) > 0.5
    full = dot(tall.astype(jnp.bfloat16), spread)
    pick = hot((full > 0.5) & (((iota((tokens, tokens), 0) ^ iota((tokens, tokens), 1)) & 15) == 0))
    got_k = pages[:, 0 : CAP * PAGE, :].reshape(tokens, HEAD)
    got_v = pages[:, CAP * PAGE : 2 * CAP * PAGE, :].reshape(tokens, HEAD)
    new = dot(pick, jnp.concatenate([got_k, got_v], axis=1))
    pool_out[0] = jnp.where(replaced, new[:, 0:HEAD], pool[0].astype(jnp.float32)).astype(jnp.bfloat16)
    pool_out[1] = jnp.where(replaced, new[:, HEAD:], pool[1].astype(jnp.float32)).astype(jnp.bfloat16)

    split_queries(q_ref, qs)
    k = jnp.concatenate([pool_out[0], fresh[0]], axis=0)
    v = jnp.concatenate([pool_out[1], fresh[1]], axis=0)
    k2 = jnp.concatenate([k, k], axis=1)
    v2 = jnp.concatenate([v, jnp.ones_like(v)], axis=1)
    scores, weights = {}, {}
    for t in range(HEADS + 2):
        if t < HEADS:
            scores[t] = lax.dot_general(
                qs[t * TOK : (t + 1) * TOK, :], k2, (((1,), (1,)), ((), ())), preferred_element_type=jnp.float32
            )
        if 0 <= t - 1 < HEADS:
            s = scores.pop(t - 1) + bias[...]
            weights[t - 1] = jnp.exp2(s - jnp.max(s, axis=1, keepdims=True)).astype(jnp.bfloat16)
        if 0 <= t - 2 < HEADS:
            o = dot(weights.pop(t - 2), v2)
            attn[:, (t - 2) * HEAD : (t - 1) * HEAD] = (o[:, 0:HEAD] / o[:, HEAD:]).astype(jnp.bfloat16)

    share = rows // 4
    part = lambda hi, lo: attn[pl.ds(pl.multiple_of((hi * 2 + lo) * share, share), share), :]
    rows_in = jnp.concatenate([part(1 - far, 1 - core), part(far, 1 - core), part(1 - far, core), part(far, core)])
    stores = []
    for t in range(TILES):
        loads[t].wait()
        cols = pl.ds(t * wide, wide)
        o_s[:, t * wide : (t + 1) * wide] = dot(rows_in, w_s[:, t * wide : (t + 1) * wide]).astype(jnp.bfloat16)
        for i, ref in enumerate((theirs, mine)):
            stores.append(
                pltpu.make_async_copy(
                    o_s.at[pl.ds(i * 2 * share, 2 * share), cols], ref.at[:, cols], sems.at[TILES + 2 * t + i]
                )
            )
            stores[-1].start()
    for store in stores:
        store.wait()


def decode(pages, perm, bias, q, fresh, pool, weight):
    rows = q.shape[0]
    keys = pool.shape[1] + rows
    depth, width = weight.shape
    return pl.pallas_call(
        decode_kernel,
        out_shape=(
            jax.ShapeDtypeStruct((rows // 2, width), jnp.bfloat16),
            jax.ShapeDtypeStruct((rows // 2, width), jnp.bfloat16),
            jax.ShapeDtypeStruct(pool.shape, jnp.bfloat16),
        ),
        in_specs=[VMEM] * 6 + [ANY],
        out_specs=(ANY, ANY, VMEM),
        scratch_shapes=[
            pltpu.VMEM((depth, width), jnp.bfloat16),
            pltpu.VMEM((rows, width), jnp.bfloat16),
            pltpu.VMEM((HEADS * rows, 2 * HEAD), jnp.bfloat16),
            pltpu.VMEM(q.shape, jnp.bfloat16),
            pltpu.SemaphoreType.DMA((3 * TILES,)),
        ],
        compiler_params=pltpu.CompilerParams(vmem_limit_bytes=VMEM_BYTES),
        cost_estimate=pl.CostEstimate(
            flops=100 * rows * depth * width,
            bytes_accessed=300 * 2**20,
            transcendentals=HEADS * rows * keys,
        ),
        name="decode",
    )(pages, perm, bias, q, fresh, pool, weight)


def body(
    q_pre,
    prefill_key_value,
    kv_past,
    offset,
    page_dest,
    slot_perm,
    pool,
    tables,
    lengths,
    decode_query,
    decode_key_value,
    out_weight,
):

    rows_dev, steps = decode_query.shape[0], decode_query.shape[1]
    rows = rows_dev * steps
    bias = make_bias(tables.T, lengths, steps)
    dec_q = decode_query.reshape(rows, -1)
    fresh = decode_key_value.reshape(2, rows, HEAD)

    outgoing, pack = prep(prefill_key_value, kv_past, page_dest)
    pages = lax.all_to_all(outgoing, "ctx", split_axis=0, concat_axis=0, tiled=True)
    near = jnp.stack([pack, send(pack, "x", 1)])
    arrays = (near, send(near, "y", 1), send(near, "y", -1), send(near, "y", 2))
    q_below, q_above, q_far = send(q_pre, "z", 1), send(q_pre, "z", -1), send(q_pre, "z", 2)

    theirs, mine, new_pool = decode(pages, slot_perm, bias, dec_q, fresh, pool, out_weight)
    f32 = jnp.float32
    share = rows // 4

    o_above = flash(offset, q_above, arrays, 1, deps=(theirs, q_far))
    o_above, theirs = lax.optimization_barrier((o_above, theirs))
    p_above = send(o_above, "z", 1)
    got = lax.ppermute(theirs, "tp", [(0, 1), (1, 0), (2, 3), (3, 2)])
    o_far = flash(offset, q_far, arrays, 2, deps=(o_above,))
    p_far = send(o_far, "z", 2)
    away = (mine[:share].astype(f32) + got[:share].astype(f32)).astype(jnp.bfloat16)
    back = lax.ppermute(away, "tp", [(0, 2), (1, 3), (2, 0), (3, 1)])
    o_below = flash(offset, q_below, arrays, 3, deps=(o_far, away))
    p_below = send(o_below, "z", -1)
    o_own = flash(offset, q_pre, arrays, 0, deps=(o_below,))
    pre_out = combine([o_own, p_above, p_far, p_below])

    dec_out = (mine[share:].astype(f32) + got[share:].astype(f32) + back.astype(f32)).astype(jnp.bfloat16)
    dec_out = dec_out.reshape(share // steps, steps, -1)
    return (pre_out, new_pool, dec_out)


def solution(mesh):
    return jax.shard_map(
        body,
        mesh=mesh,
        in_specs=(
            P("ctx", "tp"),
            P(None, "ctx", "tp"),
            P(None, "ctx", "tp"),
            P(),
            P("ctx", None),
            P("ctx", None),
            P(None, "ctx", "tp"),
            P("ctx", None),
            P("ctx", None),
            P("ctx", None, "tp"),
            P(None, "ctx", None, "tp"),
            P("tp", None),
        ),
        out_specs=(P("ctx", "tp"), P(None, "ctx", "tp"), P(("ctx", "tp"), None, None)),
        check_vma=False,
    )
```

```python
import functools

import jax
import jax.numpy as jnp
from jax import lax
from jax.experimental import pallas as pl
from jax.experimental.pallas import tpu as pltpu
from jax.sharding import PartitionSpec as P

HEAD = 128
PAGE = 16
CAP = 2
N_CTX = 32
HEADS = 8
POOL_SLOTS = 64
TOK = 256
CHUNKS = 8
SCALE = (HEAD**-0.5) * 1.4426950408889634
NEG = -1e30
SIZES = (7, 8)
VMEM_BYTES = 56 * 2**20

SMEM = pl.BlockSpec(memory_space=pltpu.SMEM)
VMEM = pl.BlockSpec(memory_space=pltpu.VMEM)
ANY = pl.BlockSpec(memory_space=pl.ANY)


def shift_perm(axis, step):
    pairs = []
    for i in range(N_CTX):
        x, y, z = i // 16, (i // 4) % 4, i % 4
        if axis == "x":
            x = (x + step) % 2
        elif axis == "y":
            y = (y + step) % 4
        else:
            z = (z + step) % 4
        pairs.append((i, x * 16 + y * 4 + z))
    return pairs


def send(v, axis, step):
    return lax.ppermute(v, "ctx", shift_perm(axis, step))


def iota(shape, dim):
    return lax.broadcasted_iota(jnp.int32, shape, dim)


def hot(mask):
    return jnp.where(mask, 1.0, 0.0).astype(jnp.bfloat16)


def dot(a, b):
    return jnp.dot(a, b, preferred_element_type=jnp.float32)


def prep_kernel(kv, past, dest_row, out, pack):
    pack[0] = kv[...]
    pack[1] = past[...]
    pages = dest_row.shape[1]
    hits = jnp.where(iota((N_CTX, pages), 0) == dest_row[...], 1.0, 0.0)
    before = hot(iota((pages, pages), 0) < iota((pages, pages), 1))
    rank = jnp.sum(hits * dot(hits.astype(jnp.bfloat16), before), axis=0, keepdims=True)
    key = dest_row[...].astype(jnp.float32) * CAP + rank
    key = jnp.broadcast_to(key, (8, pages)).astype(jnp.bfloat16)
    tokens = pages * PAGE
    spread = hot((iota((pages, tokens), 1) >> 4) == iota((pages, tokens), 0))
    target = dot(key, spread)[0:1, :] * PAGE + ((iota((1, tokens), 1) & 15)).astype(jnp.float32)
    rows = N_CTX * CAP * PAGE
    pick = hot(iota((rows, tokens), 0).astype(jnp.float32) == target)
    both = dot(pick, jnp.concatenate([kv[0], kv[1]], axis=1)).astype(jnp.bfloat16)
    out[:, 0 : CAP * PAGE, :] = both[:, 0:HEAD].reshape(N_CTX, CAP * PAGE, HEAD)
    out[:, CAP * PAGE : 2 * CAP * PAGE, :] = both[:, HEAD:].reshape(N_CTX, CAP * PAGE, HEAD)
    count = jnp.broadcast_to(jnp.sum(hits, axis=1, keepdims=True), (N_CTX, HEAD)).astype(jnp.bfloat16)
    repeat = hot((iota((N_CTX * PAGE, N_CTX), 0) >> 4) == iota((N_CTX * PAGE, N_CTX), 1))
    out[:, 2 * CAP * PAGE :, :] = dot(repeat, count).astype(jnp.bfloat16).reshape(N_CTX, PAGE, HEAD)


def prep(kv, past, page_dest):
    return pl.pallas_call(
        prep_kernel,
        out_shape=(
            jax.ShapeDtypeStruct((N_CTX, (2 * CAP + 1) * PAGE, HEAD), jnp.bfloat16),
            jax.ShapeDtypeStruct((2,) + kv.shape, jnp.bfloat16),
        ),
        in_specs=[VMEM] * 3,
        out_specs=(VMEM, VMEM),
        compiler_params=pltpu.CompilerParams(vmem_limit_bytes=VMEM_BYTES),
        name="prep",
    )(kv, past, page_dest.reshape(1, -1))


def split_queries(q_ref, qs):
    for h in range(HEADS):
        scaled = q_ref[:, h * HEAD : (h + 1) * HEAD].astype(jnp.float32) * SCALE
        high = scaled.astype(jnp.bfloat16)
        qs[h * TOK : (h + 1) * TOK, 0:HEAD] = high
        qs[h * TOK : (h + 1) * TOK, HEAD:] = (scaled - high.astype(jnp.float32)).astype(jnp.bfloat16)


def fold(qs, m_s, acc_s, k, v, ones, mask=None):
    k2 = jnp.concatenate([k, k], axis=1)
    v2 = jnp.concatenate([v, ones], axis=1)

    def score(h):
        s = lax.dot_general(
            qs[h * TOK : (h + 1) * TOK, :], k2, (((1,), (1,)), ((), ())), preferred_element_type=jnp.float32
        )
        if mask is None:
            return s
        return jnp.concatenate([jnp.where(mask, s[:, :TOK], NEG), s[:, TOK:]], axis=1)

    def soft(h, s):
        rows = slice(h * TOK, (h + 1) * TOK)
        old = m_s[rows, :]
        new = jnp.maximum(old, jnp.max(s, axis=1, keepdims=True))
        m_s[rows, :] = new
        return jnp.exp2(s - new[:, 0:1]).astype(jnp.bfloat16), jnp.exp2(old - new)

    def add(h, p, a):
        rows = slice(h * TOK, (h + 1) * TOK)
        acc_s[rows, :] = acc_s[rows, :] * jnp.concatenate([a, a], axis=1) + dot(p, v2)

    scores, weights = {}, {}
    for t in range(HEADS + 2):
        if t < HEADS:
            scores[t] = score(t)
        if 0 <= t - 1 < HEADS:
            weights[t - 1] = soft(t - 1, scores.pop(t - 1))
        if 0 <= t - 2 < HEADS:
            add(t - 2, *weights.pop(t - 2))


def flash_kernel(dz, n_dep, offset_ref, q_ref, near, plus, minus, far, *refs):
    out, q_s, k_s, v_s, ones_s, qs, m_s, acc_s, sems = refs[n_dep:]
    me, offset = lax.axis_index("ctx"), offset_ref[0]
    x, y, z = me >> 4, (me >> 2) & 3, me & 3
    group = me >> 2
    zq = (z + dz) & 3
    get_q = pltpu.make_async_copy(q_ref, q_s, sems.at[4 * CHUNKS])
    get_q.start()
    seen = group + (1 if dz == 0 else (z < zq).astype(jnp.int32))
    count = seen * TOK
    copies = []
    for s in (0, 1):
        for array, dy in ((near, 0), (plus, 3), (minus, 1), (far, 2)):
            for dx in range(2):
                j = (x ^ dx) * 4 + ((y + dy) & 3)
                if s == 0:
                    slot = jnp.where(j == group, 0, j + 1) if dz == 0 else j
                    live = slot < seen if dz else j <= group
                else:
                    length = jnp.clip(offset - (j * 4 + z) * TOK, 0, TOK)
                    count = count + length
                    slot = seen + j
                    live = length > 0
                row = pl.multiple_of(slot * TOK, TOK)
                n = len(copies)
                kc = pltpu.make_async_copy(array.at[dx, s, 0], k_s.at[pl.ds(row, TOK)], sems.at[2 * n])
                vc = pltpu.make_async_copy(array.at[dx, s, 1], v_s.at[pl.ds(row, TOK)], sems.at[2 * n + 1])
                copies.append((live, kc, vc))

                @pl.when(live)
                def _():
                    kc.start()
                    vc.start()

    ones_s[...] = jnp.ones_like(ones_s)
    m_s[...] = jnp.full_like(m_s, NEG)
    acc_s[...] = jnp.zeros_like(acc_s)
    get_q.wait()
    split_queries(q_s, qs)
    for live, kc, vc in copies:

        @pl.when(live)
        def _():
            kc.wait()
            vc.wait()

    size = jnp.int32(SIZES[-1])
    for chunks in SIZES[-2::-1]:
        size = jnp.where(count <= 2 * TOK * chunks, chunks, size)

    def fill(c, _):
        inside = iota((TOK, HEAD), 0) < count - c * TOK
        rows = pl.ds(pl.multiple_of(c * TOK, TOK), TOK)
        first = k_s[0:16, :][0:1, :].astype(jnp.float32)
        k_s[rows, :] = jnp.where(inside, k_s[rows, :].astype(jnp.float32), first).astype(jnp.bfloat16)
        v_s[rows, :] = jnp.where(inside, v_s[rows, :].astype(jnp.float32), 0.0).astype(jnp.bfloat16)
        ones_s[rows, :] = jnp.where(inside, 1.0, 0.0).astype(jnp.bfloat16)
        return 0

    lax.fori_loop(count >> 8, 2 * size, fill, 0)
    diagonal = iota((TOK, TOK), 1) <= iota((TOK, TOK), 0)

    def step(i, _):
        for chunks in SIZES:

            @pl.when(size == chunks)
            def _():
                rows = pl.ds(pl.multiple_of(i * (chunks * TOK), TOK), chunks * TOK)
                mask = diagonal | (i > 0) if dz == 0 else None
                fold(qs, m_s, acc_s, k_s[rows, :], v_s[rows, :], ones_s[rows, :], mask)

        return 0

    lax.fori_loop(0, 2, step, 0)

    lane = iota((TOK, HEAD), 1)
    level = jnp.zeros((TOK, HEAD), jnp.float32)
    for h in range(HEADS):
        rows = slice(h * TOK, (h + 1) * TOK)
        total = acc_s[rows, HEAD:]
        out[:, h * HEAD : (h + 1) * HEAD] = (acc_s[rows, 0:HEAD] / total).astype(jnp.bfloat16)
        value = m_s[rows, :] + jnp.log2(total)
        high = value.astype(jnp.bfloat16).astype(jnp.float32)
        middle = (value - high).astype(jnp.bfloat16).astype(jnp.float32)
        low = value - high - middle
        level = jnp.where(lane == h, high, level)
        level = jnp.where(lane == HEADS + h, middle, level)
        level = jnp.where(lane == 2 * HEADS + h, low, level)
    out[:, HEADS * HEAD :] = level.astype(jnp.bfloat16)


def flash(offset, q, arrays, dz, deps=()):
    work = 2 * CHUNKS * TOK * TOK * HEADS
    rows = 2 * CHUNKS * TOK
    return pl.pallas_call(
        functools.partial(flash_kernel, dz, len(deps)),
        out_shape=jax.ShapeDtypeStruct((TOK, HEADS * HEAD + HEAD), jnp.bfloat16),
        in_specs=[SMEM] + [ANY] * (5 + len(deps)),
        out_specs=VMEM,
        scratch_shapes=[
            pltpu.VMEM((TOK, HEADS * HEAD), jnp.bfloat16),
            pltpu.VMEM((rows, HEAD), jnp.bfloat16),
            pltpu.VMEM((rows, HEAD), jnp.bfloat16),
            pltpu.VMEM((rows, HEAD), jnp.bfloat16),
            pltpu.VMEM((HEADS * TOK, 2 * HEAD), jnp.bfloat16),
            pltpu.VMEM((HEADS * TOK, HEAD), jnp.float32),
            pltpu.VMEM((HEADS * TOK, 2 * HEAD), jnp.float32),
            pltpu.SemaphoreType.DMA((4 * CHUNKS + 1,)),
        ],
        compiler_params=pltpu.CompilerParams(vmem_limit_bytes=32 * 2**20),
        cost_estimate=pl.CostEstimate(flops=work * HEAD * 8, bytes_accessed=3 * 2**20, transcendentals=work),
        name=f"flash{dz}",
    )(offset, q, *arrays, *deps)


def combine_kernel(*refs):
    sources, out, held, sems = refs[:-3], refs[-3], refs[-2], refs[-1]
    copies = [pltpu.make_async_copy(source, held.at[i], sems.at[i]) for i, source in enumerate(sources)]
    for copy in copies:
        copy.start()
    for copy in copies:
        copy.wait()
    parts = [held.at[i] for i in range(len(sources))]
    width = HEADS * HEAD
    levels = []
    for part in parts:
        three = part[:, width:].astype(jnp.float32)
        levels.append(three[:, 0:HEADS] + three[:, HEADS : 2 * HEADS] + three[:, 2 * HEADS : 3 * HEADS])
    top = functools.reduce(jnp.maximum, levels)
    shares = [jnp.exp2(v - top) for v in levels]
    total = functools.reduce(jnp.add, shares)
    shares = [s / total for s in shares]
    for h in range(HEADS):
        cols = slice(h * HEAD, (h + 1) * HEAD)
        acc = jnp.zeros((TOK, HEAD), jnp.float32)
        for part, share in zip(parts, shares):
            acc = acc + part[:, cols].astype(jnp.float32) * share[:, h : h + 1]
        out[:, cols] = acc.astype(jnp.bfloat16)


def combine(parts):
    return pl.pallas_call(
        combine_kernel,
        out_shape=jax.ShapeDtypeStruct((TOK, HEADS * HEAD), jnp.bfloat16),
        in_specs=[ANY] * len(parts),
        out_specs=VMEM,
        scratch_shapes=[
            pltpu.VMEM((len(parts),) + parts[0].shape, jnp.bfloat16),
            pltpu.SemaphoreType.DMA((len(parts),)),
        ],
        compiler_params=pltpu.CompilerParams(vmem_limit_bytes=16 * 2**20),
        name="combine",
    )(*parts)


TILES = 4


def bias_kernel(table, length, out):
    pages, rows = table.shape
    slots, steps = POOL_SLOTS, out.shape[0] // rows
    tokens, all_rows = slots * PAGE, rows * steps
    live = length[...]
    whole = live >> 4
    slot_id = iota((slots, rows), 0)
    times = jnp.zeros((slots, rows), jnp.float32)
    ending = jnp.zeros((slots, rows), jnp.float32)
    for a in range(pages):
        hit = table[a : a + 1, :] == slot_id
        times = times + jnp.where(hit & (whole > a), 1.0, 0.0)
        ending = ending + jnp.where(hit & (whole == a), 1.0, 0.0)
    repeat = hot(iota((rows, all_rows), 0) == (iota((rows, all_rows), 1) >> 2))
    spread = hot((iota((slots, tokens), 1) >> 4) == iota((slots, tokens), 0))
    rest = jnp.broadcast_to((live & 15).astype(jnp.float32), (8, rows)).astype(jnp.bfloat16)
    rest = dot(rest, repeat)[0:1, :]
    r, c = iota((all_rows, all_rows), 0), iota((all_rows, all_rows), 1)
    rest = jnp.sum(jnp.where(r == c, rest, 0.0), axis=1, keepdims=True)

    def widen(v):
        v = dot(v.astype(jnp.bfloat16), repeat).astype(jnp.bfloat16)
        return lax.dot_general(v, spread, (((0,), (0,)), ((), ())), preferred_element_type=jnp.float32)

    in_page = ((iota((all_rows, tokens), 1) & 15)).astype(jnp.float32)
    count = widen(times) + jnp.where(in_page < rest, widen(ending), 0.0)
    out[:, 0:tokens] = jnp.where(count > 0.5, jnp.log2(jnp.maximum(count, 1.0)), NEG)
    out[:, tokens:] = jnp.where(((r >> 2) == (c >> 2)) & (c <= r), 0.0, NEG)


def make_bias(table, length, steps):
    rows = table.shape[1]
    return pl.pallas_call(
        bias_kernel,
        out_shape=jax.ShapeDtypeStruct((rows * steps, POOL_SLOTS * PAGE + rows * steps), jnp.float32),
        in_specs=[VMEM] * 2,
        out_specs=VMEM,
        compiler_params=pltpu.CompilerParams(vmem_limit_bytes=VMEM_BYTES),
        name="bias",
    )(table, length)


def decode_kernel(pages, perm, bias, q_ref, fresh, pool, weight, theirs, mine, pool_out, *scratch):
    w_s, o_s, qs, attn, sems = scratch
    tp = lax.axis_index("tp")
    core, far = tp & 1, tp >> 1
    rows = q_ref.shape[0]
    wide = w_s.shape[1] // TILES
    loads = []
    for t in range(TILES):
        cols = pl.ds(t * wide, wide)
        loads.append(pltpu.make_async_copy(weight.at[:, cols], w_s.at[:, cols], sems.at[t]))
        loads[-1].start()

    slots = perm.shape[1]
    flags = pages[:, 2 * CAP * PAGE :, :].reshape(N_CTX * PAGE, HEAD)
    first = hot(iota((N_CTX, N_CTX * PAGE), 1) == iota((N_CTX, N_CTX * PAGE), 0) * PAGE)
    sent = dot(first, flags)[:, 0:slots]
    lane = iota((N_CTX, slots), 1)
    there = ((lane >> 1) == iota((N_CTX, slots), 0)) & (sent > (lane & 1).astype(jnp.float32) + 0.5)
    there = jnp.sum(jnp.where(there, 1.0, 0.0), axis=0, keepdims=True)
    earlier = hot(iota((slots, slots), 0) < iota((slots, slots), 1))
    rank = dot(jnp.broadcast_to(there, (8, slots)).astype(jnp.bfloat16), earlier)[0:1, :]
    by_rank = hot((iota((slots, slots), 0).astype(jnp.float32) == rank) & (there > 0.5))
    by_slot = hot(iota((slots, slots), 0) == perm[...])
    moves = dot(by_slot, by_rank).astype(jnp.bfloat16)
    tokens = slots * PAGE
    spread = hot((iota((slots, tokens), 1) >> 4) == iota((slots, tokens), 0))
    spread_t = hot((iota((tokens, slots), 0) >> 4) == iota((tokens, slots), 1))
    tall = dot(spread_t, moves)
    replaced = jnp.sum(tall, axis=1, keepdims=True) > 0.5
    full = dot(tall.astype(jnp.bfloat16), spread)
    pick = hot((full > 0.5) & (((iota((tokens, tokens), 0) ^ iota((tokens, tokens), 1)) & 15) == 0))
    got_k = pages[:, 0 : CAP * PAGE, :].reshape(tokens, HEAD)
    got_v = pages[:, CAP * PAGE : 2 * CAP * PAGE, :].reshape(tokens, HEAD)
    new = dot(pick, jnp.concatenate([got_k, got_v], axis=1))
    pool_out[0] = jnp.where(replaced, new[:, 0:HEAD], pool[0].astype(jnp.float32)).astype(jnp.bfloat16)
    pool_out[1] = jnp.where(replaced, new[:, HEAD:], pool[1].astype(jnp.float32)).astype(jnp.bfloat16)

    split_queries(q_ref, qs)
    k = jnp.concatenate([pool_out[0], fresh[0]], axis=0)
    v = jnp.concatenate([pool_out[1], fresh[1]], axis=0)
    k2 = jnp.concatenate([k, k], axis=1)
    v2 = jnp.concatenate([v, jnp.ones_like(v)], axis=1)
    scores, weights = {}, {}
    for t in range(HEADS + 2):
        if t < HEADS:
            scores[t] = lax.dot_general(
                qs[t * TOK : (t + 1) * TOK, :], k2, (((1,), (1,)), ((), ())), preferred_element_type=jnp.float32
            )
        if 0 <= t - 1 < HEADS:
            s = scores.pop(t - 1) + bias[...]
            weights[t - 1] = jnp.exp2(s - jnp.max(s, axis=1, keepdims=True)).astype(jnp.bfloat16)
        if 0 <= t - 2 < HEADS:
            o = dot(weights.pop(t - 2), v2)
            attn[:, (t - 2) * HEAD : (t - 1) * HEAD] = (o[:, 0:HEAD] / o[:, HEAD:]).astype(jnp.bfloat16)

    share = rows // 4
    part = lambda hi, lo: attn[pl.ds(pl.multiple_of((hi * 2 + lo) * share, share), share), :]
    rows_in = jnp.concatenate([part(1 - far, 1 - core), part(far, 1 - core), part(1 - far, core), part(far, core)])
    stores = []
    for t in range(TILES):
        loads[t].wait()
        cols = pl.ds(t * wide, wide)
        o_s[:, t * wide : (t + 1) * wide] = dot(rows_in, w_s[:, t * wide : (t + 1) * wide]).astype(jnp.bfloat16)
        for i, ref in enumerate((theirs, mine)):
            stores.append(
                pltpu.make_async_copy(
                    o_s.at[pl.ds(i * 2 * share, 2 * share), cols], ref.at[:, cols], sems.at[TILES + 2 * t + i]
                )
            )
            stores[-1].start()
    for store in stores:
        store.wait()


def decode(pages, perm, bias, q, fresh, pool, weight):
    rows = q.shape[0]
    keys = pool.shape[1] + rows
    depth, width = weight.shape
    return pl.pallas_call(
        decode_kernel,
        out_shape=(
            jax.ShapeDtypeStruct((rows // 2, width), jnp.bfloat16),
            jax.ShapeDtypeStruct((rows // 2, width), jnp.bfloat16),
            jax.ShapeDtypeStruct(pool.shape, jnp.bfloat16),
        ),
        in_specs=[VMEM] * 6 + [ANY],
        out_specs=(ANY, ANY, VMEM),
        scratch_shapes=[
            pltpu.VMEM((depth, width), jnp.bfloat16),
            pltpu.VMEM((rows, width), jnp.bfloat16),
            pltpu.VMEM((HEADS * rows, 2 * HEAD), jnp.bfloat16),
            pltpu.VMEM(q.shape, jnp.bfloat16),
            pltpu.SemaphoreType.DMA((3 * TILES,)),
        ],
        compiler_params=pltpu.CompilerParams(vmem_limit_bytes=VMEM_BYTES),
        cost_estimate=pl.CostEstimate(
            flops=100 * rows * depth * width,
            bytes_accessed=300 * 2**20,
            transcendentals=HEADS * rows * keys,
        ),
        name="decode",
    )(pages, perm, bias, q, fresh, pool, weight)


def body(
    q_pre,
    prefill_key_value,
    kv_past,
    offset,
    page_dest,
    slot_perm,
    pool,
    tables,
    lengths,
    decode_query,
    decode_key_value,
    out_weight,
):

    rows_dev, steps = decode_query.shape[0], decode_query.shape[1]
    rows = rows_dev * steps
    bias = make_bias(tables.T, lengths, steps)
    dec_q = decode_query.reshape(rows, -1)
    fresh = decode_key_value.reshape(2, rows, HEAD)

    outgoing, pack = prep(prefill_key_value, kv_past, page_dest)
    pages = lax.all_to_all(outgoing, "ctx", split_axis=0, concat_axis=0, tiled=True)
    near = jnp.stack([pack, send(pack, "x", 1)])
    arrays = (near, send(near, "y", 1), send(near, "y", -1), send(near, "y", 2))
    q_below, q_above, q_far = send(q_pre, "z", 1), send(q_pre, "z", -1), send(q_pre, "z", 2)

    theirs, mine, new_pool = decode(pages, slot_perm, bias, dec_q, fresh, pool, out_weight)
    f32 = jnp.float32
    share = rows // 4

    o_above = flash(offset, q_above, arrays, 1, deps=(theirs, q_far))
    o_above, theirs = lax.optimization_barrier((o_above, theirs))
    p_above = send(o_above, "z", 1)
    got = lax.ppermute(theirs, "tp", [(0, 1), (1, 0), (2, 3), (3, 2)])
    o_far = flash(offset, q_far, arrays, 2, deps=(o_above,))
    p_far = send(o_far, "z", 2)
    away = (mine[:share].astype(f32) + got[:share].astype(f32)).astype(jnp.bfloat16)
    back = lax.ppermute(away, "tp", [(0, 2), (1, 3), (2, 0), (3, 1)])
    o_below = flash(offset, q_below, arrays, 3, deps=(o_far, away))
    p_below = send(o_below, "z", -1)
    o_own = flash(offset, q_pre, arrays, 0, deps=(o_below,))
    pre_out = combine([o_own, p_above, p_far, p_below])

    dec_out = (mine[share:].astype(f32) + got[share:].astype(f32) + back.astype(f32)).astype(jnp.bfloat16)
    dec_out = dec_out.reshape(share // steps, steps, -1)
    return (pre_out, new_pool, dec_out)


def solution(mesh):
    return jax.shard_map(
        body,
        mesh=mesh,
        in_specs=(
            P("ctx", "tp"),
            P(None, "ctx", "tp"),
            P(None, "ctx", "tp"),
            P(),
            P("ctx", None),
            P("ctx", None),
            P(None, "ctx", "tp"),
            P("ctx", None),
            P("ctx", None),
            P("ctx", None, "tp"),
            P(None, "ctx", None, "tp"),
            P("tp", None),
        ),
        out_specs=(P("ctx", "tp"), P(None, "ctx", "tp"), P(("ctx", "tp"), None, None)),
        check_vma=False,
    )
```
